256 devices in a mesh: bucket: 64 (over z, y_lo, x), span: 4 (over y_hi, core).
Axes of the slice: x: 4, y: 4 (y_hi: 2, y_lo: 2; y = y_hi * 2 + y_lo), z: 8, core: 2. Of those that a mesh axis runs over, the one named last changes fastest.
Arguments:
- left_emb: bfloat16 [400, 65536], P(None, 'bucket'), may hold values from -1.5 to 1.5
- right_emb: bfloat16 [400, 65536], P(None, 'bucket'), may hold values from -1.5 to 1.5
- relation_weight: float32 [400, 16], replicated, may hold values from -6 to 6
- left_index: int32 [64, 4, 1024], P('bucket', 'span'), may hold values from 0 to 1023
- right_index: int32 [64, 4, 1024], P('bucket', 'span'), may hold values from 0 to 1023
- relation_index: int32 [64, 4, 1024], P('bucket', 'span'), may hold values from 0 to 15
- edge_count: int32 [64, 4], P('bucket', 'span'), may hold values from 1 to 1024, 2048 in all within a row
- neg_index: int32 [64, 1000], P('bucket'), may hold values from 0 to 1023
Outputs:
- left_grad: float32 [400, 65536], P(None, ('bucket', 'span'))
- right_grad: float32 [400, 65536], P(None, ('bucket', 'span'))
- relation_grad: float32 [400, 16], replicated
The draws below stay inside these ranges and needn't reach their ends.
Inputs may be any that keep to these rules, and one draw needn't show every extreme that they name: `edge_count`: the 4 counts of one bucket sum to 2048, and in every bucket one of them equals 1024.
All inputs are finite; a program needn't handle non-finite values. No bound on the sum of `edge_count` on one device may be relied on, other than what follows from the above.
Results may differ from the reference program's by a relative error of at most 0.0033.
Values may be sent and summed in bfloat16 or wider, within the bound.
A program may use at most 64 MiB of HBM per device.

```python
import math
import jax
import jax.numpy as jnp
import numpy as np
from jax import lax

D = 400
NEG = 1000
REL = 16
PART = 1024
EDGE_DEV = 1024
NP = 65536
N_BUCKET = 64
N_SPAN = 4


def plant(array, key, low, high):
    place = [jax.random.randint(jax.random.fold_in(key, axis), (), 0, length) for axis, length in enumerate(array.shape)]
    longest = array.shape.index(max(array.shape))
    next_to = place[:longest] + [(place[longest] + 1) % array.shape[longest]] + place[longest + 1:]
    return array.at[tuple(place)].set(low).at[tuple(next_to)].set(high)


def block_scale(own_key, dims, split, low, top_value):
    def one(position, parts):
        heights = jax.random.uniform(jax.random.fold_in(jax.random.fold_in(own_key, 6), position), (parts,), jnp.float32, low / len(split), top_value / len(split))
        return jnp.repeat(jnp.exp(heights), dims[position] // parts).reshape((-1,) + (1,) * (len(dims) - position - 1))

    level = one(*split[0])
    for cut in split[1:]:
        level = level * one(*cut)
    return level


def profile(number_of, total, bound, slope):
    weights = [(1 << 20) // math.isqrt(grade ** slope) + 1 for grade in range(2, number_of + 1)]
    surplus, holding = total - bound - (number_of - 1), [1] * (number_of - 1)
    while surplus > 0:
        movable = [i for i in range(number_of - 1) if holding[i] < bound]
        whole, budget = sum([weights[i] for i in movable]), surplus
        for i in movable:
            more = min(bound - holding[i], max(1, budget * weights[i] // whole), surplus)
            holding[i] = holding[i] + more
            surplus = surplus - more
    return np.array([bound] + holding)


def ragged(stream_key, number_of, total, bound, skew):
    if number_of == 2:
        one = jax.random.randint(stream_key, (), max(1, total - bound), min(bound, total - 1) + 1)
        return jnp.stack([one, total - one])
    sizes = jnp.asarray(profile(number_of, total, bound, skew), jnp.int32)
    twos = (number_of - 1) // 2
    source_of, taker = sizes[1:1 + 2 * twos:2], sizes[2:2 + 2 * twos:2]
    slack = jnp.minimum(source_of - 1, bound - taker)
    passed = jax.random.randint(jax.random.fold_in(stream_key, 1), (twos,), 0, 1 << 20) % (slack + 1)
    sizes = sizes.at[1:1 + 2 * twos:2].set(source_of - passed).at[2:2 + 2 * twos:2].set(taker + passed)
    return sizes[jax.random.permutation(jax.random.fold_in(stream_key, 2), number_of)]


def scatter_about(own_key, extent, deviation, limit, pieces=(), held_as=jnp.bfloat16):
    result = deviation * jax.random.normal(own_key, extent, jnp.float32)
    if pieces:
        result = result * block_scale(own_key, extent, pieces, -0.22, 0.18)
    return jnp.clip(result, -limit, limit).astype(held_as)


def setup_inputs(seed: int = 0) -> dict:
    streams_of = jax.random.split(jax.random.key(seed), 9)
    left_emb = scatter_about(streams_of[0], (D, NP), 0.25, 1.5, ((1, 64),))
    right_emb = scatter_about(streams_of[1], (D, NP), 0.25, 1.5, ((1, 64),))
    relation_weight = scatter_about(streams_of[2], (D, REL), 1.0, 6.0, (), jnp.float32)
    left_index = plant(jax.random.randint(streams_of[3], (N_BUCKET, N_SPAN, EDGE_DEV), 0, PART), jax.random.fold_in(streams_of[3], 1), 0, PART - 1).astype(jnp.int32)
    right_index = plant(jax.random.randint(streams_of[4], (N_BUCKET, N_SPAN, EDGE_DEV), 0, PART), jax.random.fold_in(streams_of[4], 1), 0, PART - 1).astype(jnp.int32)
    relation_index = plant(jax.random.randint(streams_of[5], (N_BUCKET, N_SPAN, EDGE_DEV), 0, REL), jax.random.fold_in(streams_of[5], 1), 0, REL - 1).astype(jnp.int32)
    edge_count = jax.vmap(lambda own: ragged(own, N_SPAN, 2 * EDGE_DEV, EDGE_DEV, 2))(jax.random.split(streams_of[6], N_BUCKET)).reshape((N_BUCKET, N_SPAN)).astype(jnp.int32)
    neg_index = plant(jax.random.randint(streams_of[7], (N_BUCKET, NEG), 0, PART), jax.random.fold_in(streams_of[7], 1), 0, PART - 1).astype(jnp.int32)
    return {"left_emb": left_emb, "right_emb": right_emb, "relation_weight": relation_weight, "left_index": left_index, "right_index": right_index, "relation_index": relation_index, "edge_count": edge_count, "neg_index": neg_index}


def make_query(relation_cols, right_values, half_width, axis):
    rot_real = lax.slice_in_dim(relation_cols, 0, half_width, axis=axis)
    rot_imag = lax.slice_in_dim(relation_cols, half_width, 2 * half_width, axis=axis)
    right_real = lax.slice_in_dim(right_values, 0, half_width, axis=axis)
    right_imag = lax.slice_in_dim(right_values, half_width, 2 * half_width, axis=axis)
    return jnp.concatenate([rot_real * right_real + rot_imag * right_imag, rot_real * right_imag - rot_imag * right_real], axis)


def wide_dot(first, second):
    return jnp.dot(first.astype(jnp.float32), second.astype(jnp.float32), precision=lax.Precision.HIGHEST, preferred_element_type=jnp.float32)


def bucket_gradients(left_part, right_part, relation_weight, left_cols, right_cols, relation_ids, negatives):
    width = left_part.shape[0]
    half_width = width // 2
    left_table = left_part.T.astype(jnp.float32)
    right_table = right_part.T.astype(jnp.float32)
    left_rows = jnp.take(left_table, left_cols, axis=0)
    right_values = jnp.take(right_table, right_cols, axis=0)
    relation_rows = jnp.take(relation_weight.T, relation_ids, axis=0)
    query_short = make_query(relation_rows, right_values, half_width, 1).astype(jnp.bfloat16)
    query_values = query_short.astype(jnp.float32)
    positive = jnp.sum(left_rows * query_values, 1)
    pos_weight = -jax.nn.sigmoid(-positive)
    negative_rows = jnp.take(left_table, negatives, axis=0)
    scores = wide_dot(query_values, negative_rows.T)
    neg_weight = (jax.nn.sigmoid(scores) / NEG).astype(jnp.bfloat16)
    query_grad = left_rows * pos_weight[:, None] + wide_dot(neg_weight, negative_rows)
    neg_total = wide_dot(neg_weight.T, query_values)
    grad_real = query_grad[:, :half_width]
    grad_imag = query_grad[:, half_width:]
    rot_real = relation_rows[:, :half_width]
    rot_imag = relation_rows[:, half_width:]
    right_real = right_values[:, :half_width]
    right_imag = right_values[:, half_width:]
    right_rows_grad = jnp.concatenate([grad_real * rot_real - grad_imag * rot_imag, grad_real * rot_imag + grad_imag * rot_real], 1)
    rotation_grad = jnp.concatenate([grad_real * right_real + grad_imag * right_imag, grad_real * right_imag - grad_imag * right_real], 1)
    left_rows_total = jnp.zeros((left_part.shape[1], width), jnp.float32).at[left_cols].add(query_values * pos_weight[:, None])
    left_total = left_rows_total.at[negatives].add(neg_total).T
    right_total = jnp.zeros((right_part.shape[1], width), jnp.float32).at[right_cols].add(right_rows_grad).T
    relation_total = jnp.zeros((relation_weight.shape[1], width), jnp.float32).at[relation_ids].add(rotation_grad).T
    return left_total, right_total, relation_total


def reference(left_emb, right_emb, relation_weight, left_index, right_index, relation_index, edge_count, neg_index):
    width = left_emb.shape[0]

    def one_bucket(running, bucket):
        left_part = lax.dynamic_slice_in_dim(left_emb, bucket * PART, PART, 1)
        source = (bucket + N_BUCKET - 1) % N_BUCKET
        right_part = lax.dynamic_slice_in_dim(right_emb, source * PART, PART, 1)
        span_counts = edge_count[bucket].astype(jnp.int32)
        count_ends = jnp.cumsum(span_counts).astype(jnp.int32)
        count_starts = (count_ends - span_counts).astype(jnp.int32)
        rank_list = jnp.arange(2 * EDGE_DEV, dtype=jnp.int32)
        owner_span = jnp.sum((rank_list[:, None] >= count_ends[None, :-1]).astype(jnp.int32), 1).astype(jnp.int32)
        flat_slot = (owner_span * EDGE_DEV + rank_list - count_starts[owner_span]).astype(jnp.int32)
        left_cols = left_index[bucket].reshape(-1)[flat_slot]
        right_cols = right_index[bucket].reshape(-1)[flat_slot]
        relation_ids = relation_index[bucket].reshape(-1)[flat_slot]
        left_total, right_total, relation_total = bucket_gradients(left_part, right_part, relation_weight, left_cols, right_cols, relation_ids, neg_index[bucket])
        return running + relation_total, (left_total, right_total)

    relation_grad, stacked = lax.scan(one_bucket, jnp.zeros((width, REL), jnp.float32), jnp.arange(N_BUCKET, dtype=jnp.int32))
    left_stack, right_stack = stacked
    right_stack = jnp.roll(right_stack, -1, axis=0)
    left_grad = jnp.transpose(left_stack, (1, 0, 2)).reshape(width, N_BUCKET * PART)
    right_grad = jnp.transpose(right_stack, (1, 0, 2)).reshape(width, N_BUCKET * PART)
    return left_grad, right_grad, relation_grad
```

```python
import functools
import math

import jax
import jax.numpy as jnp
from jax import lax
from jax.experimental import pallas as pl
from jax.experimental.pallas import tpu as pltpu
from jax.sharding import PartitionSpec as P

MESH = pl.DeviceIdType.MESH
CHUNKS = 4
TILE = 256
F32 = jnp.float32
BF16 = jnp.bfloat16


def nt_dot(a, b):
    return lax.dot_general(a, b, (((1,), (1,)), ((), ())), preferred_element_type=F32)


def dot(a, b):
    return jnp.dot(a, b, preferred_element_type=F32)


def kernel(
    inner,
    left_hbm,
    right_hbm,
    relw_hbm,
    lidx_hbm,
    ridx_hbm,
    relidx_hbm,
    count_hbm,
    neg_hbm,
    left_out,
    right_out,
    rel_out,
    left,
    left_t,
    relw,
    wcat,
    own_idx,
    own_count,
    neg,
    cnt,
    idx_buf,
    edges,
    rbuf,
    query_s,
    w_tile,
    w_own,
    rrg_hi,
    rrg_lo,
    rel_acc,
    back_send,
    back_recv,
    left_stage,
    rb1,
    rb2,
    rb3,
    load_sem,
    idx_send,
    idx_recv,
    fwd_send,
    fwd_recv,
    pass_send,
    back_ssem,
    back_rsem,
    r1_send,
    r1_recv,
    r2_send,
    r2_recv,
    r3_send,
    r3_recv,
    out_sem,
):
    width, part = left.shape
    half = width // 2
    n_bucket = lax.axis_size("bucket")
    n_span = lax.axis_size("span")
    outer = n_bucket // inner
    b = lax.axis_index("bucket")
    s = lax.axis_index("span")
    count_neg = neg.shape[1]
    total_edges = edges.shape[1]
    slots = own_idx.shape[2]
    own_width = part // n_span
    chunk = part // CHUNKS
    core = lax.rem(s, 2)
    sibling = s + 1 - 2 * core
    nxt = lax.rem(b + 1, n_bucket)
    prv = lax.rem(b + n_bucket - 1, n_bucket)
    j = lax.rem(b, inner)
    zi = lax.div(b, inner)

    loads = [
        pltpu.make_async_copy(src, dst, load_sem.at[i])
        for i, (src, dst) in enumerate(
            [
                (lidx_hbm.at[0], own_idx.at[0]),
                (ridx_hbm.at[0], own_idx.at[1]),
                (relidx_hbm.at[0], own_idx.at[2]),
                (count_hbm, own_count),
                (neg_hbm, neg),
                (relw_hbm, relw),
                (left_hbm, left),
            ]
        )
    ]
    for load in loads:
        load.start()

    barrier = pltpu.get_barrier_semaphore()
    peers = [(nxt, s), (prv, s)]
    span_peers = [(b, lax.rem(s + d, n_span)) for d in range(1, n_span)]
    inner_peers = [(zi * inner + lax.rem(j + d, inner), s) for d in range(1, inner)]
    outer_peers = [(lax.rem(zi + d, outer) * inner + j, s) for d in range(1, outer)]
    peers = peers + span_peers + inner_peers + outer_peers
    for peer in peers:
        pl.semaphore_signal(barrier, inc=1, device_id=peer, device_id_type=MESH)
    pl.semaphore_wait(barrier, len(peers))

    fwd = []
    for i in range(CHUNKS // 2):
        k = core * (CHUNKS // 2) + i
        fwd.append(
            pltpu.make_async_remote_copy(
                src_ref=right_hbm.at[:, pl.ds(pl.multiple_of(k * chunk, chunk), chunk)],
                dst_ref=rbuf.at[k],
                send_sem=fwd_send.at[i],
                recv_sem=fwd_recv.at[k],
                device_id=(nxt, s),
                device_id_type=MESH,
            )
        )
        fwd[-1].start()

    for load in loads[:4]:
        load.wait()
    slot = lax.broadcasted_iota(jnp.int32, (1, slots), 1)
    live = slot < own_count[...]
    idx_buf[s, 0:1, :] = jnp.where(live, own_idx[0], -1)
    idx_buf[s, 1:2, :] = own_idx[1]
    idx_buf[s, 2:3, :] = own_idx[2]
    idx_buf[s, 3:4, :] = jnp.zeros((1, slots), jnp.int32)
    idx_copies = []
    for d, peer in enumerate(span_peers):
        idx_copies.append(
            pltpu.make_async_remote_copy(
                src_ref=idx_buf.at[s],
                dst_ref=idx_buf.at[s],
                send_sem=idx_send.at[d],
                recv_sem=idx_recv.at[s],
                device_id=peer,
                device_id_type=MESH,
            )
        )
        idx_copies[-1].start()

    loads[4].wait()
    for k in range(part // 128):
        col = lax.broadcasted_iota(jnp.int32, (128, count_neg), 0) + k * 128
        hits = jnp.where(col == neg[...], 1.0, 0.0).astype(F32)
        times = jnp.sum(hits, axis=1, keepdims=True) * (1.0 / count_neg)
        cnt[k * 128 : (k + 1) * 128, :] = jnp.broadcast_to(times, (128, 128))

    loads[5].wait()
    rel_count = relw.shape[1]
    w0 = relw[...]
    w_hi = w0.astype(BF16)
    w1 = w0 - w_hi.astype(F32)
    w_mid = w1.astype(BF16)
    w_lo = (w1 - w_mid.astype(F32)).astype(BF16)
    row = lax.broadcasted_iota(jnp.int32, (rel_count, 128), 0)
    lane = lax.broadcasted_iota(jnp.int32, (rel_count, 128), 1)
    placed = jnp.zeros((width, 128), F32)
    for t, term in enumerate((w_hi, w_mid, w_lo)):
        put = jnp.where(lane == row + t * rel_count, 1.0, 0.0).astype(BF16)
        placed = placed + dot(term, put)
    wcat[...] = placed.astype(BF16)

    loads[6].wait()
    for k in range(part // 128):
        block = left[:, k * 128 : (k + 1) * 128].astype(F32)
        left_t[k * 128 : (k + 1) * 128, :] = block.T.astype(BF16)

    for d in range(1, n_span):
        c = lax.rem(s + d, n_span)
        pltpu.make_async_remote_copy(
            src_ref=idx_buf.at[c],
            dst_ref=idx_buf.at[c],
            send_sem=idx_send.at[d - 1],
            recv_sem=idx_recv.at[c],
            device_id=(b, c),
            device_id_type=MESH,
        ).wait_recv()
    rank = lax.broadcasted_iota(jnp.int32, (4, total_edges), 1)
    packed = jnp.zeros((4, total_edges), jnp.int32)
    start = jnp.zeros((1, 1), jnp.int32)
    for c in range(n_span):
        value = idx_buf[c]
        alive = jnp.where(value[0:1, :] >= 0, 1.0, 0.0).astype(F32)
        size = jnp.sum(alive, axis=1, keepdims=True).astype(jnp.int32)
        value = jnp.concatenate([value, jnp.zeros((4, total_edges - slots), jnp.int32)], axis=1)
        if c > 0:
            for bit in range((total_edges - 1).bit_length()):
                moved = pltpu.roll(value, 1 << bit, 1)
                on = jnp.broadcast_to(start & (1 << bit), (4, total_edges)) != 0
                value = jnp.where(on, moved, value)
        inside = (rank >= start) & (rank < start + size)
        packed = jnp.where(inside, value, packed)
        start = start + size
    edges[...] = packed

    passes = []
    for i in range(CHUNKS // 2):
        k = core * (CHUNKS // 2) + i
        fwd[i].wait_recv()
        passes.append(
            pltpu.make_async_remote_copy(
                src_ref=rbuf.at[k],
                dst_ref=rbuf.at[k],
                send_sem=pass_send.at[i],
                recv_sem=fwd_recv.at[k],
                device_id=(b, sibling),
                device_id_type=MESH,
            )
        )
        passes[-1].start()
    for i in range(CHUNKS // 2):
        k = (1 - core) * (CHUNKS // 2) + i
        pltpu.make_async_remote_copy(
            src_ref=rbuf.at[k],
            dst_ref=rbuf.at[k],
            send_sem=pass_send.at[i],
            recv_sem=fwd_recv.at[k],
            device_id=(b, sibling),
            device_id_type=MESH,
        ).wait_recv()

    rel_acc[...] = jnp.zeros_like(rel_acc)
    own_start = pl.multiple_of(s * own_width, own_width)

    def tile_step(t, _):
        at = pl.ds(pl.multiple_of(t * TILE, TILE), TILE)
        l_row = edges[0:1, at]
        r_row = edges[1:2, at]
        t_row = edges[2:3, at]
        right_rows = jnp.zeros((width, TILE), F32)
        for k in range(CHUNKS):
            col = lax.broadcasted_iota(jnp.int32, (chunk, TILE), 0) + k * chunk
            pick = jnp.where(col == r_row, 1.0, 0.0).astype(BF16)
            right_rows = right_rows + dot(rbuf[k], pick)
        kind = lax.broadcasted_iota(jnp.int32, (128, TILE), 0)
        pick_rel = jnp.where((kind & (rel_count - 1)) == t_row, 1.0, 0.0).astype(BF16)
        rot = dot(wcat[...], pick_rel)
        w_re, w_im = rot[:half], rot[half:]
        r_re, r_im = right_rows[:half], right_rows[half:]
        query = jnp.concatenate(
            [w_re * r_re + w_im * r_im, w_re * r_im - w_im * r_re], axis=0
        ).astype(BF16)
        query_s[:, at] = query
        scores = dot(left_t[...], query)
        col = lax.broadcasted_iota(jnp.int32, (part, TILE), 0)
        is_left = col == l_row
        positive = jnp.sum(jnp.where(is_left, scores, 0.0), axis=0, keepdims=True)
        pos_weight = -1.0 / (1.0 + jnp.exp(positive))
        times = cnt[...]
        times = jnp.concatenate([times] * (TILE // 128), axis=1)
        weight = times / (1.0 + jnp.exp(-scores))
        weight = (weight + jnp.where(is_left, pos_weight, 0.0)).astype(BF16)
        w_tile[...] = weight
        w_own[:, at] = w_tile[pl.ds(own_start, own_width), :]
        grad = dot(left[...], weight)
        a, c = grad[:half], grad[half:]
        rows = jnp.concatenate([a * w_re - c * w_im, a * w_im + c * w_re], axis=0)
        hi = rows.astype(BF16)
        rrg_hi[:, at] = hi
        rrg_lo[:, at] = (rows - hi.astype(F32)).astype(BF16)
        turn = jnp.concatenate([a * r_re + c * r_im, a * r_im - c * r_re], axis=0).astype(BF16)
        own_kind = lax.broadcasted_iota(jnp.int32, (16, TILE), 0) + s * (rel_count // n_span)
        pick_own = jnp.where(own_kind == t_row, 1.0, 0.0).astype(BF16)
        rel_acc[...] += nt_dot(pick_own, turn)
        return 0

    lax.fori_loop(0, total_edges // TILE, tile_step, 0)

    def exchange(buf, me, peers, slots_of, send_sem, recv_sem):
        copies = []
        for d, (peer, other) in enumerate(zip(peers, slots_of)):
            copies.append(
                (
                    pltpu.make_async_remote_copy(
                        src_ref=buf.at[me],
                        dst_ref=buf.at[me],
                        send_sem=send_sem.at[d],
                        recv_sem=recv_sem.at[me],
                        device_id=peer,
                        device_id_type=MESH,
                    ),
                    pltpu.make_async_remote_copy(
                        src_ref=buf.at[other],
                        dst_ref=buf.at[other],
                        send_sem=send_sem.at[d],
                        recv_sem=recv_sem.at[other],
                        device_id=peer,
                        device_id_type=MESH,
                    ),
                )
            )
            copies[-1][0].start()
        return copies

    rel_rows = rel_count // n_span
    rb1[j] = rel_acc[0:rel_rows, :]
    stage1 = exchange(
        rb1, j, inner_peers, [lax.rem(j + d, inner) for d in range(1, inner)], r1_send, r1_recv
    )

    r_all = edges[1:2, :]
    col = lax.broadcasted_iota(jnp.int32, (own_width, total_edges), 0) + s * own_width
    pick = jnp.where(col == r_all, 1.0, 0.0).astype(BF16)
    right_own = nt_dot(rrg_hi[...], pick) + nt_dot(rrg_lo[...], pick)
    back_send[...] = right_own.astype(BF16)
    back = pltpu.make_async_remote_copy(
        src_ref=back_send,
        dst_ref=back_recv,
        send_sem=back_ssem,
        recv_sem=back_rsem,
        device_id=(prv, s),
        device_id_type=MESH,
    )
    back.start()

    for _, incoming in stage1:
        incoming.wait_recv()
    rb2[zi] = jnp.sum(rb1[...], axis=0)
    stage2 = exchange(
        rb2, zi, outer_peers, [lax.rem(zi + d, outer) for d in range(1, outer)], r2_send, r2_recv
    )

    left_stage[...] = nt_dot(query_s[...], w_own[...])
    left_copy = pltpu.make_async_copy(left_stage, left_out, out_sem.at[0])
    left_copy.start()

    for _, incoming in stage2:
        incoming.wait_recv()
    rb3[s] = jnp.sum(rb2[...], axis=0)
    stage3 = exchange(
        rb3, s, span_peers, [lax.rem(s + d, n_span) for d in range(1, n_span)], r3_send, r3_recv
    )
    for _, incoming in stage3:
        incoming.wait_recv()
    rel_copy = pltpu.make_async_copy(rb3, rel_out, out_sem.at[2])
    rel_copy.start()

    back.wait_recv()
    right_copy = pltpu.make_async_copy(back_recv, right_out, out_sem.at[1])
    right_copy.start()

    for copy in fwd + idx_copies + passes:
        copy.wait_send()
    back.wait_send()
    for stage in (stage1, stage2, stage3):
        for outgoing, _ in stage:
            outgoing.wait_send()
    left_copy.wait()
    rel_copy.wait()
    right_copy.wait()


def solution(mesh):
    n_bucket = mesh.shape["bucket"]
    n_span = mesh.shape["span"]
    inner = math.isqrt(n_bucket)
    outer = n_bucket // inner

    def per_device(
        left_emb,
        right_emb,
        relation_weight,
        left_index,
        right_index,
        relation_index,
        edge_count,
        neg_index,
    ):
        width, part = left_emb.shape
        slots = left_index.shape[2]
        total_edges = 2 * slots
        own = part // n_span
        rel_count = relation_weight.shape[1]
        rel_rows = rel_count // n_span
        any_space = pl.BlockSpec(memory_space=pl.ANY)
        dma = pltpu.SemaphoreType.DMA
        left_grad, right_grad, rel_grad = pl.pallas_call(
            functools.partial(kernel, inner),
            out_shape=(
                jax.ShapeDtypeStruct((width, own), F32),
                jax.ShapeDtypeStruct((width, own), BF16),
                jax.ShapeDtypeStruct((n_span, rel_rows, width), F32),
            ),
            in_specs=[any_space] * 8,
            out_specs=[any_space] * 3,
            scratch_shapes=[
                pltpu.VMEM((width, part), BF16),
                pltpu.VMEM((part, width), BF16),
                pltpu.VMEM((width, rel_count), F32),
                pltpu.VMEM((width, 128), BF16),
                pltpu.VMEM((3, 1, slots), jnp.int32),
                pltpu.VMEM((1, 1), jnp.int32),
                pltpu.VMEM((1, neg_index.shape[1]), jnp.int32),
                pltpu.VMEM((part, 128), F32),
                pltpu.VMEM((n_span, 4, slots), jnp.int32),
                pltpu.VMEM((4, total_edges), jnp.int32),
                pltpu.VMEM((CHUNKS, width, part // CHUNKS), BF16),
                pltpu.VMEM((width, total_edges), BF16),
                pltpu.VMEM((part, TILE), BF16),
                pltpu.VMEM((own, total_edges), BF16),
                pltpu.VMEM((width, total_edges), BF16),
                pltpu.VMEM((width, total_edges), BF16),
                pltpu.VMEM((16, width), F32),
                pltpu.VMEM((width, own), BF16),
                pltpu.VMEM((width, own), BF16),
                pltpu.VMEM((width, own), F32),
                pltpu.VMEM((inner, rel_rows, width), F32),
                pltpu.VMEM((outer, rel_rows, width), F32),
                pltpu.VMEM((n_span, rel_rows, width), F32),
                dma((7,)),
                dma((n_span - 1,)),
                dma((n_span,)),
                dma((CHUNKS // 2,)),
                dma((CHUNKS,)),
                dma((CHUNKS // 2,)),
                dma,
                dma,
                dma((inner,)),
                dma((inner,)),
                dma((outer,)),
                dma((outer,)),
                dma((n_span,)),
                dma((n_span,)),
                dma((3,)),
            ],
            compiler_params=pltpu.CompilerParams(
                collective_id=0, has_side_effects=True, vmem_limit_bytes=48 * 1024 * 1024
            ),
        )(
            left_emb,
            right_emb,
            relation_weight,
            left_index,
            right_index,
            relation_index,
            edge_count,
            neg_index,
        )
        rel_grad = rel_grad.reshape(rel_count, width).T
        return left_grad, right_grad.astype(F32), rel_grad

    in_specs = (
        P(None, "bucket"),
        P(None, "bucket"),
        P(),
        P("bucket", "span", None),
        P("bucket", "span", None),
        P("bucket", "span", None),
        P("bucket", "span"),
        P("bucket", None),
    )
    out_specs = (P(None, ("bucket", "span")), P(None, ("bucket", "span")), P())
    return jax.shard_map(
        per_device, mesh=mesh, in_specs=in_specs, out_specs=out_specs, check_vma=False
    )
```

```python
import functools
import math

import jax
import jax.numpy as jnp
from jax import lax
from jax.experimental import pallas as pl
from jax.experimental.pallas import tpu as pltpu
from jax.sharding import PartitionSpec as P

MESH = pl.DeviceIdType.MESH
CHUNKS = 4
TILE = 512
F32 = jnp.float32
BF16 = jnp.bfloat16


def nt_dot(a, b):
    return lax.dot_general(a, b, (((1,), (1,)), ((), ())), preferred_element_type=F32)


def dot(a, b):
    return jnp.dot(a, b, preferred_element_type=F32)


def kernel(
    inner,
    left_hbm,
    right_hbm,
    relw_hbm,
    lidx_hbm,
    ridx_hbm,
    relidx_hbm,
    count_hbm,
    neg_hbm,
    left_out,
    right_out,
    rel_out,
    left,
    left_t,
    relw,
    wcat,
    own_idx,
    own_count,
    neg,
    cnt,
    idx_buf,
    edges,
    rbuf,
    query_s,
    w_s,
    rrg_hi,
    rrg_lo,
    rel_acc,
    back_send,
    left_stage,
    right_rows_s,
    rel_part,
    right_part,
    left_part,
    rb1,
    rb2,
    rb3,
    load_sem,
    idx_send,
    idx_recv,
    fwd_send,
    fwd_recv,
    pass_send,
    back_ssem,
    back_rsem,
    part_send,
    part_recv,
    r1_send,
    r1_recv,
    r2_send,
    r2_recv,
    r3_send,
    r3_recv,
    out_sem,
):
    width, part = left.shape
    half = width // 2
    n_bucket = lax.axis_size("bucket")
    n_span = lax.axis_size("span")
    outer = n_bucket // inner
    b = lax.axis_index("bucket")
    s = lax.axis_index("span")
    count_neg = neg.shape[1]
    total_edges = edges.shape[1]
    slots = own_idx.shape[2]
    own_width = part // n_span
    chunk = part // CHUNKS
    core = lax.rem(s, 2)
    sibling = s + 1 - 2 * core
    nxt = lax.rem(b + 1, n_bucket)
    prv = lax.rem(b + n_bucket - 1, n_bucket)
    j = lax.rem(b, inner)
    zi = lax.div(b, inner)

    barrier = pltpu.get_barrier_semaphore()
    peers = [(nxt, s), (prv, s)]
    span_peers = [(b, lax.rem(s + d, n_span)) for d in range(1, n_span)]
    inner_peers = [(zi * inner + lax.rem(j + d, inner), s) for d in range(1, inner)]
    outer_peers = [(lax.rem(zi + d, outer) * inner + j, s) for d in range(1, outer)]
    peers = peers + span_peers + inner_peers + outer_peers
    for peer in peers:
        pl.semaphore_signal(barrier, inc=1, device_id=peer, device_id_type=MESH)
    loads = [
        pltpu.make_async_copy(src, dst, load_sem.at[i])
        for i, (src, dst) in enumerate(
            [
                (lidx_hbm.at[0], own_idx.at[0]),
                (ridx_hbm.at[0], own_idx.at[1]),
                (relidx_hbm.at[0], own_idx.at[2]),
                (count_hbm, own_count),
                (neg_hbm, neg),
                (relw_hbm, relw),
                (left_hbm, left),
            ]
        )
    ]
    for load in loads:
        load.start()

    for load in loads[:4]:
        load.wait()
    slot = lax.broadcasted_iota(jnp.int32, (1, slots), 1)
    live = slot < own_count[...]
    idx_buf[s, 0:1, :] = jnp.where(live, own_idx[0], -1)
    idx_buf[s, 1:2, :] = own_idx[1]
    idx_buf[s, 2:3, :] = own_idx[2]
    idx_buf[s, 3:4, :] = jnp.zeros((1, slots), jnp.int32)

    pl.semaphore_wait(barrier, len(peers))

    idx_copies = []
    for d, peer in enumerate(span_peers):
        idx_copies.append(
            pltpu.make_async_remote_copy(
                src_ref=idx_buf.at[s],
                dst_ref=idx_buf.at[s],
                send_sem=idx_send.at[d],
                recv_sem=idx_recv.at[s],
                device_id=peer,
                device_id_type=MESH,
            )
        )
        idx_copies[-1].start()

    fwd = []
    for i in range(CHUNKS // 2):
        k = core * (CHUNKS // 2) + i
        fwd.append(
            pltpu.make_async_remote_copy(
                src_ref=right_hbm.at[:, pl.ds(pl.multiple_of(k * chunk, chunk), chunk)],
                dst_ref=rbuf.at[k],
                send_sem=fwd_send.at[i],
                recv_sem=fwd_recv.at[k],
                device_id=(nxt, s),
                device_id_type=MESH,
            )
        )
        fwd[-1].start()

    loads[4].wait()
    for k in range(part // 128):
        col = lax.broadcasted_iota(jnp.int32, (128, count_neg), 0) + k * 128
        hits = jnp.where(col == neg[...], 1.0, 0.0).astype(F32)
        times = jnp.sum(hits, axis=1, keepdims=True) * (1.0 / count_neg)
        cnt[k * 128 : (k + 1) * 128, :] = jnp.broadcast_to(times, (128, 128))

    loads[5].wait()
    rel_count = relw.shape[0]
    w0 = relw[...]
    w_hi = w0.astype(BF16).astype(F32)
    w_mid = (w0 - w_hi).astype(BF16).astype(F32)
    w_lo = w0 - w_hi - w_mid
    blank = jnp.zeros((128 - 3 * rel_count, width), F32)
    wcat[...] = jnp.concatenate([w_hi, w_mid, w_lo, blank], axis=0).T.astype(BF16)

    loads[6].wait()
    for k in range(part // 128):
        block = left[:, k * 128 : (k + 1) * 128].astype(F32)
        left_t[k * 128 : (k + 1) * 128, :] = block.T.astype(BF16)

    for d in range(1, n_span):
        c = lax.rem(s + d, n_span)
        pltpu.make_async_remote_copy(
            src_ref=idx_buf.at[c],
            dst_ref=idx_buf.at[c],
            send_sem=idx_send.at[d - 1],
            recv_sem=idx_recv.at[c],
            device_id=(b, c),
            device_id_type=MESH,
        ).wait_recv()
    rank = lax.broadcasted_iota(jnp.int32, (4, total_edges), 1)
    packed = jnp.zeros((4, total_edges), jnp.int32)
    start = jnp.zeros((1, 1), jnp.int32)
    for c in range(n_span):
        value = idx_buf[c]
        alive = jnp.where(value[0:1, :] >= 0, 1.0, 0.0).astype(F32)
        size = jnp.sum(alive, axis=1, keepdims=True).astype(jnp.int32)
        value = jnp.concatenate([value, jnp.zeros((4, total_edges - slots), jnp.int32)], axis=1)
        if c > 0:
            for bit in range((total_edges - 1).bit_length()):
                moved = pltpu.roll(value, 1 << bit, 1)
                on = jnp.broadcast_to(start & (1 << bit), (4, total_edges)) != 0
                value = jnp.where(on, moved, value)
        inside = (rank >= start) & (rank < start + size)
        packed = jnp.where(inside, value, packed)
        start = start + size
    edges[...] = packed

    core_edges = total_edges // 2
    first = core * core_edges

    def gather(k, fresh):
        for t in range(core_edges // TILE):
            r_row = edges[1:2, pl.ds(pl.multiple_of(first + t * TILE, TILE), TILE)]
            col = lax.broadcasted_iota(jnp.int32, (chunk, TILE), 0) + k * chunk
            pick = jnp.where(col == r_row, 1.0, 0.0).astype(BF16)
            found = dot(rbuf[k], pick)
            at = slice(t * TILE, (t + 1) * TILE)
            right_rows_s[:, at] = found if fresh else right_rows_s[:, at] + found

    passes = []
    for i in range(CHUNKS // 2):
        k = core * (CHUNKS // 2) + i
        fwd[i].wait_recv()
        passes.append(
            pltpu.make_async_remote_copy(
                src_ref=rbuf.at[k],
                dst_ref=rbuf.at[k],
                send_sem=pass_send.at[i],
                recv_sem=fwd_recv.at[k],
                device_id=(b, sibling),
                device_id_type=MESH,
            )
        )
        passes[-1].start()
        gather(k, i == 0)
    for i in range(CHUNKS // 2):
        k = (1 - core) * (CHUNKS // 2) + i
        pltpu.make_async_remote_copy(
            src_ref=rbuf.at[k],
            dst_ref=rbuf.at[k],
            send_sem=pass_send.at[i],
            recv_sem=fwd_recv.at[k],
            device_id=(b, sibling),
            device_id_type=MESH,
        ).wait_recv()
        gather(k, False)

    rel_acc[...] = jnp.zeros_like(rel_acc)
    own_start = pl.multiple_of(s * own_width, own_width)
    sib_start = pl.multiple_of(sibling * own_width, own_width)
    chip_kind = (s - core) * (rel_count // n_span)

    def tile_step(t):
        at = slice(t * TILE, (t + 1) * TILE)
        edge_at = pl.ds(pl.multiple_of(first + t * TILE, TILE), TILE)
        l_row = edges[0:1, edge_at]
        t_row = edges[2:3, edge_at]
        right_rows = right_rows_s[:, at]
        kind = lax.broadcasted_iota(jnp.int32, (128, TILE), 0)
        pick_rel = jnp.where((kind & (rel_count - 1)) == t_row, 1.0, 0.0).astype(BF16)
        rot = dot(wcat[...], pick_rel)
        w_re, w_im = rot[:half], rot[half:]
        r_re, r_im = right_rows[:half], right_rows[half:]
        query = jnp.concatenate(
            [w_re * r_re + w_im * r_im, w_re * r_im - w_im * r_re], axis=0
        ).astype(BF16)
        query_s[:, at] = query
        scores = dot(left_t[...], query)
        col = lax.broadcasted_iota(jnp.int32, (part, TILE), 0)
        is_left = col == l_row
        positive = jnp.sum(jnp.where(is_left, scores, 0.0), axis=0, keepdims=True)
        pos_weight = -1.0 / (1.0 + jnp.exp(positive))
        times = cnt[...]
        times = jnp.concatenate([times] * (TILE // 128), axis=1)
        weight = times * pl.reciprocal(1.0 + jnp.exp(-scores), approx=True)
        weight = (weight + jnp.where(is_left, pos_weight, 0.0)).astype(BF16)
        w_s[:, at] = weight
        grad = dot(left[...], weight)
        a, c = grad[:half], grad[half:]
        rows = jnp.concatenate([a * w_re - c * w_im, a * w_im + c * w_re], axis=0)
        hi = rows.astype(BF16)
        rrg_hi[:, at] = hi
        rrg_lo[:, at] = (rows - hi.astype(F32)).astype(BF16)
        turn = jnp.concatenate([a * r_re + c * r_im, a * r_im - c * r_re], axis=0).astype(BF16)
        own_kind = lax.broadcasted_iota(jnp.int32, (16, TILE), 0) + chip_kind
        pick_own = jnp.where(own_kind == t_row, 1.0, 0.0).astype(BF16)
        rel_acc[...] += nt_dot(pick_own, turn)

    for t in range(core_edges // TILE):
        tile_step(t)

    def exchange(buf, me, peers, slots_of, send_sem, recv_sem):
        copies = []
        for d, (peer, other) in enumerate(zip(peers, slots_of)):
            copies.append(
                (
                    pltpu.make_async_remote_copy(
                        src_ref=buf.at[me],
                        dst_ref=buf.at[me],
                        send_sem=send_sem.at[d],
                        recv_sem=recv_sem.at[me],
                        device_id=peer,
                        device_id_type=MESH,
                    ),
                    pltpu.make_async_remote_copy(
                        src_ref=buf.at[other],
                        dst_ref=buf.at[other],
                        send_sem=send_sem.at[d],
                        recv_sem=recv_sem.at[other],
                        device_id=peer,
                        device_id_type=MESH,
                    ),
                )
            )
            copies[-1][0].start()
        return copies

    def to_sibling(i, src, dst):
        copy = pltpu.make_async_remote_copy(
            src_ref=src,
            dst_ref=dst,
            send_sem=part_send.at[i],
            recv_sem=part_recv.at[i],
            device_id=(b, sibling),
            device_id_type=MESH,
        )
        copy.start()
        return copy

    rel_rows = rel_count // n_span
    rel_part[0, 0] = rel_acc[0:rel_rows, :]
    rel_part[0, 1] = rel_acc[rel_rows : 2 * rel_rows, :]
    rel_half = to_sibling(0, rel_part.at[0, 1 - core], rel_part.at[1, 0])

    r_own = edges[1:2, pl.ds(pl.multiple_of(first, core_edges), core_edges)]

    def right_columns(start):
        col = lax.broadcasted_iota(jnp.int32, (own_width, core_edges), 0) + start
        pick = jnp.where(col == r_own, 1.0, 0.0).astype(BF16)
        return nt_dot(rrg_hi[...], pick) + nt_dot(rrg_lo[...], pick)

    def left_columns(start):
        return nt_dot(query_s[...], w_s[pl.ds(start, own_width), :])

    right_part[0] = right_columns(sib_start)
    right_half = to_sibling(1, right_part.at[0], right_part.at[1])

    rel_half.wait_recv()
    rb1[j] = rel_part[0, core] + rel_part[1, 0]
    stage1 = exchange(
        rb1, j, inner_peers, [lax.rem(j + d, inner) for d in range(1, inner)], r1_send, r1_recv
    )

    right_own = right_columns(own_start)
    right_half.wait_recv()
    back_send[...] = (right_own + right_part[1]).astype(BF16)
    back = pltpu.make_async_remote_copy(
        src_ref=back_send,
        dst_ref=right_out,
        send_sem=back_ssem,
        recv_sem=back_rsem,
        device_id=(prv, s),
        device_id_type=MESH,
    )
    back.start()

    left_part[0] = left_columns(sib_start)
    left_half = to_sibling(2, left_part.at[0], left_part.at[1])

    for _, incoming in stage1:
        incoming.wait_recv()
    rb2[zi] = jnp.sum(rb1[...], axis=0)
    stage2 = exchange(
        rb2, zi, outer_peers, [lax.rem(zi + d, outer) for d in range(1, outer)], r2_send, r2_recv
    )

    left_own = left_columns(own_start)
    left_half.wait_recv()
    left_stage[...] = left_own + left_part[1]
    left_copy = pltpu.make_async_copy(left_stage, left_out, out_sem.at[0])
    left_copy.start()

    for _, incoming in stage2:
        incoming.wait_recv()
    rb3[...] = jnp.sum(rb2[...], axis=0)
    own_rel = pltpu.make_async_copy(rb3, rel_out.at[s], out_sem.at[1])
    own_rel.start()
    stage3 = []
    for d, (peer, other) in enumerate(
        zip(span_peers, [lax.rem(s + d, n_span) for d in range(1, n_span)])
    ):
        stage3.append(
            (
                pltpu.make_async_remote_copy(
                    src_ref=rb3,
                    dst_ref=rel_out.at[s],
                    send_sem=r3_send.at[d],
                    recv_sem=r3_recv.at[s],
                    device_id=peer,
                    device_id_type=MESH,
                ),
                pltpu.make_async_remote_copy(
                    src_ref=rb3,
                    dst_ref=rel_out.at[other],
                    send_sem=r3_send.at[d],
                    recv_sem=r3_recv.at[other],
                    device_id=peer,
                    device_id_type=MESH,
                ),
            )
        )
        stage3[-1][0].start()
    back.wait_recv()
    for _, incoming in stage3:
        incoming.wait_recv()

    for copy in fwd + idx_copies + passes:
        copy.wait_send()
    back.wait_send()
    for stage in (stage1, stage2, stage3):
        for outgoing, _ in stage:
            outgoing.wait_send()
    for copy in (rel_half, right_half, left_half):
        copy.wait_send()
    left_copy.wait()
    own_rel.wait()


def finish(left_in, right_in, rel_in, left_out, right_out, rel_out, left_v, right_b, right_f, rel_a, rel_b, sems):
    groups, rows = rel_a.shape[0], rel_a.shape[1]
    right_copy = pltpu.make_async_copy(right_in, right_b, sems.at[0])
    right_copy.start()
    rel_copy = pltpu.make_async_copy(rel_in, rel_a, sems.at[1])
    rel_copy.start()
    left_copy = pltpu.make_async_copy(left_in, left_v, sems.at[2])
    left_copy.start()
    right_copy.wait()
    right_f[...] = right_b[...].astype(F32)
    right_done = pltpu.make_async_copy(right_f, right_out, sems.at[3])
    right_done.start()
    left_copy.wait()
    left_done = pltpu.make_async_copy(left_v, left_out, sems.at[5])
    left_done.start()
    rel_copy.wait()
    for g in range(groups):
        rel_b[g * rows : (g + 1) * rows, :] = rel_a[g]
    rel_done = pltpu.make_async_copy(rel_b, rel_out, sems.at[4])
    rel_done.start()
    left_done.wait()
    right_done.wait()
    rel_done.wait()


def solution(mesh):
    n_bucket = mesh.shape["bucket"]
    n_span = mesh.shape["span"]
    inner = math.isqrt(n_bucket)
    outer = n_bucket // inner

    def per_device(
        left_emb,
        right_emb,
        relation_weight,
        left_index,
        right_index,
        relation_index,
        edge_count,
        neg_index,
    ):
        width, part = left_emb.shape
        slots = left_index.shape[2]
        total_edges = 2 * slots
        own = part // n_span
        rel_count = relation_weight.shape[1]
        rel_rows = rel_count // n_span
        any_space = pl.BlockSpec(memory_space=pl.ANY)
        dma = pltpu.SemaphoreType.DMA
        left_grad, right_grad, rel_grad = pl.pallas_call(
            functools.partial(kernel, inner),
            out_shape=(
                jax.ShapeDtypeStruct((width, own), F32),
                jax.ShapeDtypeStruct((width, own), BF16),
                jax.ShapeDtypeStruct((n_span, rel_rows, width), F32),
            ),
            in_specs=[pl.BlockSpec(memory_space=pltpu.HBM)] * 8,
            out_specs=[any_space] * 3,
            scratch_shapes=[
                pltpu.VMEM((width, part), BF16),
                pltpu.VMEM((part, width), BF16),
                pltpu.VMEM((rel_count, width), F32),
                pltpu.VMEM((width, 128), BF16),
                pltpu.VMEM((3, 1, slots), jnp.int32),
                pltpu.VMEM((1, 1), jnp.int32),
                pltpu.VMEM((1, neg_index.shape[1]), jnp.int32),
                pltpu.VMEM((part, 128), F32),
                pltpu.VMEM((n_span, 4, slots), jnp.int32),
                pltpu.VMEM((4, total_edges), jnp.int32),
                pltpu.VMEM((CHUNKS, width, part // CHUNKS), BF16),
                pltpu.VMEM((width, slots), BF16),
                pltpu.VMEM((part, slots), BF16),
                pltpu.VMEM((width, slots), BF16),
                pltpu.VMEM((width, slots), BF16),
                pltpu.VMEM((16, width), F32),
                pltpu.VMEM((width, own), BF16),
                pltpu.VMEM((width, own), F32),
                pltpu.VMEM((width, slots), F32),
                pltpu.VMEM((2, 2, rel_rows, width), F32),
                pltpu.VMEM((2, width, own), F32),
                pltpu.VMEM((2, width, own), F32),
                pltpu.VMEM((inner, rel_rows, width), F32),
                pltpu.VMEM((outer, rel_rows, width), F32),
                pltpu.VMEM((rel_rows, width), F32),
                dma((7,)),
                dma((n_span - 1,)),
                dma((n_span,)),
                dma((CHUNKS // 2,)),
                dma((CHUNKS,)),
                dma((CHUNKS // 2,)),
                dma,
                dma,
                dma((3,)),
                dma((3,)),
                dma((inner,)),
                dma((inner,)),
                dma((outer,)),
                dma((outer,)),
                dma((n_span,)),
                dma((n_span,)),
                dma((2,)),
            ],
            compiler_params=pltpu.CompilerParams(
                collective_id=0, has_side_effects=True, vmem_limit_bytes=63 * 1024 * 1024
            ),
        )(
            left_emb,
            right_emb,
            relation_weight.T,
            left_index,
            right_index,
            relation_index,
            edge_count,
            neg_index,
        )
        left_grad, right_grad, rel_grad = pl.pallas_call(
            finish,
            out_shape=(
                jax.ShapeDtypeStruct((width, own), F32),
                jax.ShapeDtypeStruct((width, own), F32),
                jax.ShapeDtypeStruct((rel_count, width), F32),
            ),
            in_specs=[any_space] * 3,
            out_specs=[any_space] * 3,
            scratch_shapes=[
                pltpu.VMEM((width, own), F32),
                pltpu.VMEM((width, own), BF16),
                pltpu.VMEM((width, own), F32),
                pltpu.VMEM((n_span, rel_rows, width), F32),
                pltpu.VMEM((rel_count, width), F32),
                dma((6,)),
            ],
        )(left_grad, right_grad, rel_grad)
        return left_grad, right_grad, rel_grad.T

    in_specs = (
        P(None, "bucket"),
        P(None, "bucket"),
        P(),
        P("bucket", "span", None),
        P("bucket", "span", None),
        P("bucket", "span", None),
        P("bucket", "span"),
        P("bucket", None),
    )
    out_specs = (P(None, ("bucket", "span")), P(None, ("bucket", "span")), P())
    return jax.shard_map(
        per_device, mesh=mesh, in_specs=in_specs, out_specs=out_specs, check_vma=False
    )
```

```python
import functools
import math

import jax
import jax.numpy as jnp
from jax import lax
from jax.experimental import pallas as pl
from jax.experimental.pallas import tpu as pltpu
from jax.sharding import PartitionSpec as P

MESH = pl.DeviceIdType.MESH
CHUNKS = 4
TILE = 512
F32 = jnp.float32
BF16 = jnp.bfloat16


def nt_dot(a, b):
    return lax.dot_general(a, b, (((1,), (1,)), ((), ())), preferred_element_type=F32)


def dot(a, b):
    return jnp.dot(a, b, preferred_element_type=F32)


def kernel(
    inner,
    left_hbm,
    right_hbm,
    relw_hbm,
    lidx_hbm,
    ridx_hbm,
    relidx_hbm,
    count_hbm,
    neg_hbm,
    left_out,
    right_out,
    rel_out,
    left,
    left_t,
    relw,
    wcat,
    own_idx,
    own_count,
    neg,
    cnt,
    idx_buf,
    edges,
    rbuf,
    query_s,
    w_s,
    rrg_hi,
    rrg_lo,
    rel_acc,
    back_send,
    left_stage,
    right_rows_s,
    rel_part,
    right_part,
    left_part,
    rb1,
    rb2,
    rb3,
    load_sem,
    idx_send,
    idx_recv,
    fwd_send,
    fwd_recv,
    pass_send,
    back_ssem,
    back_rsem,
    part_send,
    part_recv,
    r1_send,
    r1_recv,
    r2_send,
    r2_recv,
    out_sem,
):
    width, part = left.shape
    half = width // 2
    n_bucket = lax.axis_size("bucket")
    n_span = lax.axis_size("span")
    outer = n_bucket // inner
    b = lax.axis_index("bucket")
    s = lax.axis_index("span")
    count_neg = neg.shape[1]
    total_edges = edges.shape[1]
    slots = own_idx.shape[2]
    own_width = part // n_span
    chunk = part // CHUNKS
    core = lax.rem(s, 2)
    sibling = s + 1 - 2 * core
    nxt = lax.rem(b + 1, n_bucket)
    prv = lax.rem(b + n_bucket - 1, n_bucket)
    j = lax.rem(b, inner)
    zi = lax.div(b, inner)

    barrier = pltpu.get_barrier_semaphore()
    peers = [(nxt, s), (prv, s)]
    span_peers = [(b, lax.rem(s + d, n_span)) for d in range(1, n_span)]
    inner_peers = [(zi * inner + lax.rem(j + d, inner), s) for d in range(1, inner)]
    outer_peers = [(lax.rem(zi + d, outer) * inner + j, s) for d in range(1, outer)]
    peers = peers + span_peers + inner_peers + outer_peers
    for peer in peers:
        pl.semaphore_signal(barrier, inc=1, device_id=peer, device_id_type=MESH)
    loads = [
        pltpu.make_async_copy(src, dst, load_sem.at[i])
        for i, (src, dst) in enumerate(
            [
                (lidx_hbm.at[0], own_idx.at[0]),
                (ridx_hbm.at[0], own_idx.at[1]),
                (relidx_hbm.at[0], own_idx.at[2]),
                (count_hbm, own_count),
                (neg_hbm, neg),
                (relw_hbm, relw),
                (left_hbm, left),
            ]
        )
    ]
    for load in loads:
        load.start()

    pl.semaphore_wait(barrier, len(peers))

    fwd = []
    for i in range(CHUNKS // 2):
        k = core * (CHUNKS // 2) + i
        fwd.append(
            pltpu.make_async_remote_copy(
                src_ref=right_hbm.at[:, pl.ds(pl.multiple_of(k * chunk, chunk), chunk)],
                dst_ref=rbuf.at[k],
                send_sem=fwd_send.at[i],
                recv_sem=fwd_recv.at[k],
                device_id=(nxt, s),
                device_id_type=MESH,
            )
        )
        fwd[-1].start()

    for load in loads[:4]:
        load.wait()
    slot = lax.broadcasted_iota(jnp.int32, (1, slots), 1)
    live = slot < own_count[...]
    idx_buf[s, 0:1, :] = jnp.where(live, own_idx[0], -1)
    idx_buf[s, 1:2, :] = own_idx[1]
    idx_buf[s, 2:3, :] = own_idx[2]
    idx_buf[s, 3:4, :] = jnp.zeros((1, slots), jnp.int32)

    idx_copies = []
    for d, peer in enumerate(span_peers):
        idx_copies.append(
            pltpu.make_async_remote_copy(
                src_ref=idx_buf.at[s],
                dst_ref=idx_buf.at[s],
                send_sem=idx_send.at[d],
                recv_sem=idx_recv.at[s],
                device_id=peer,
                device_id_type=MESH,
            )
        )
        idx_copies[-1].start()

    loads[4].wait()
    for k in range(part // 128):
        col = lax.broadcasted_iota(jnp.int32, (128, count_neg), 0) + k * 128
        hits = jnp.where(col == neg[...], 1.0, 0.0).astype(F32)
        times = jnp.sum(hits, axis=1, keepdims=True) * (1.0 / count_neg)
        cnt[k * 128 : (k + 1) * 128, :] = jnp.broadcast_to(times, (128, 128))

    loads[5].wait()
    rel_count = relw.shape[0]
    w0 = relw[...]
    w_hi = w0.astype(BF16).astype(F32)
    w_mid = (w0 - w_hi).astype(BF16).astype(F32)
    w_lo = w0 - w_hi - w_mid
    blank = jnp.zeros((128 - 3 * rel_count, width), F32)
    wcat[...] = jnp.concatenate([w_hi, w_mid, w_lo, blank], axis=0).T.astype(BF16)

    loads[6].wait()
    for k in range(part // 128):
        block = left[:, k * 128 : (k + 1) * 128].astype(F32)
        left_t[k * 128 : (k + 1) * 128, :] = block.T.astype(BF16)

    for d in range(1, n_span):
        c = lax.rem(s + d, n_span)
        pltpu.make_async_remote_copy(
            src_ref=idx_buf.at[c],
            dst_ref=idx_buf.at[c],
            send_sem=idx_send.at[d - 1],
            recv_sem=idx_recv.at[c],
            device_id=(b, c),
            device_id_type=MESH,
        ).wait_recv()
    rank = lax.broadcasted_iota(jnp.int32, (4, total_edges), 1)
    packed = jnp.zeros((4, total_edges), jnp.int32)
    start = jnp.zeros((1, 1), jnp.int32)
    for c in range(n_span):
        value = idx_buf[c]
        alive = jnp.where(value[0:1, :] >= 0, 1.0, 0.0).astype(F32)
        size = jnp.sum(alive, axis=1, keepdims=True).astype(jnp.int32)
        value = jnp.concatenate([value, jnp.zeros((4, total_edges - slots), jnp.int32)], axis=1)
        if c > 0:
            for bit in range((total_edges - 1).bit_length()):
                moved = pltpu.roll(value, 1 << bit, 1)
                on = jnp.broadcast_to(start & (1 << bit), (4, total_edges)) != 0
                value = jnp.where(on, moved, value)
        inside = (rank >= start) & (rank < start + size)
        packed = jnp.where(inside, value, packed)
        start = start + size
    edges[...] = packed

    core_edges = total_edges // 2
    first = core * core_edges

    def gather(k, fresh):
        for t in range(core_edges // TILE):
            r_row = edges[1:2, pl.ds(pl.multiple_of(first + t * TILE, TILE), TILE)]
            col = lax.broadcasted_iota(jnp.int32, (chunk, TILE), 0) + k * chunk
            pick = jnp.where(col == r_row, 1.0, 0.0).astype(BF16)
            found = dot(rbuf[k], pick)
            at = slice(t * TILE, (t + 1) * TILE)
            right_rows_s[:, at] = found if fresh else right_rows_s[:, at] + found

    passes = []
    for i in range(CHUNKS // 2):
        k = core * (CHUNKS // 2) + i
        fwd[i].wait_recv()
        passes.append(
            pltpu.make_async_remote_copy(
                src_ref=rbuf.at[k],
                dst_ref=rbuf.at[k],
                send_sem=pass_send.at[i],
                recv_sem=fwd_recv.at[k],
                device_id=(b, sibling),
                device_id_type=MESH,
            )
        )
        passes[-1].start()
        gather(k, i == 0)
    for i in range(CHUNKS // 2):
        k = (1 - core) * (CHUNKS // 2) + i
        pltpu.make_async_remote_copy(
            src_ref=rbuf.at[k],
            dst_ref=rbuf.at[k],
            send_sem=pass_send.at[i],
            recv_sem=fwd_recv.at[k],
            device_id=(b, sibling),
            device_id_type=MESH,
        ).wait_recv()
        gather(k, False)

    rel_acc[...] = jnp.zeros_like(rel_acc)
    own_start = pl.multiple_of(s * own_width, own_width)
    sib_start = pl.multiple_of(sibling * own_width, own_width)

    def tile_step(t):
        at = slice(t * TILE, (t + 1) * TILE)
        edge_at = pl.ds(pl.multiple_of(first + t * TILE, TILE), TILE)
        l_row = edges[0:1, edge_at]
        t_row = edges[2:3, edge_at]
        right_rows = right_rows_s[:, at]
        kind = lax.broadcasted_iota(jnp.int32, (128, TILE), 0)
        pick_rel = jnp.where((kind & (rel_count - 1)) == t_row, 1.0, 0.0).astype(BF16)
        rot = dot(wcat[...], pick_rel)
        w_re, w_im = rot[:half], rot[half:]
        r_re, r_im = right_rows[:half], right_rows[half:]
        query = jnp.concatenate(
            [w_re * r_re + w_im * r_im, w_re * r_im - w_im * r_re], axis=0
        ).astype(BF16)
        query_s[:, at] = query
        scores = dot(left_t[...], query)
        col = lax.broadcasted_iota(jnp.int32, (part, TILE), 0)
        is_left = col == l_row
        positive = jnp.sum(jnp.where(is_left, scores, 0.0), axis=0, keepdims=True)
        pos_weight = -1.0 / (1.0 + jnp.exp(positive))
        times = cnt[...]
        times = jnp.concatenate([times] * (TILE // 128), axis=1)
        weight = times * pl.reciprocal(1.0 + jnp.exp(-scores), approx=True)
        weight = (weight + jnp.where(is_left, pos_weight, 0.0)).astype(BF16)
        w_s[:, at] = weight
        grad = dot(left[...], weight)
        a, c = grad[:half], grad[half:]
        rows = jnp.concatenate([a * w_re - c * w_im, a * w_im + c * w_re], axis=0)
        hi = rows.astype(BF16)
        rrg_hi[:, at] = hi
        rrg_lo[:, at] = (rows - hi.astype(F32)).astype(BF16)
        turn = jnp.concatenate([a * r_re + c * r_im, a * r_im - c * r_re], axis=0).astype(BF16)
        own_kind = lax.broadcasted_iota(jnp.int32, (rel_count, TILE), 0)
        pick_own = jnp.where(own_kind == t_row, 1.0, 0.0).astype(BF16)
        rel_acc[...] += nt_dot(pick_own, turn)

    for t in range(core_edges // TILE):
        tile_step(t)

    def exchange(buf, me, peers, slots_of, send_sem, recv_sem):
        copies = []
        for d, (peer, other) in enumerate(zip(peers, slots_of)):
            copies.append(
                (
                    pltpu.make_async_remote_copy(
                        src_ref=buf.at[me],
                        dst_ref=buf.at[me],
                        send_sem=send_sem.at[d],
                        recv_sem=recv_sem.at[me],
                        device_id=peer,
                        device_id_type=MESH,
                    ),
                    pltpu.make_async_remote_copy(
                        src_ref=buf.at[other],
                        dst_ref=buf.at[other],
                        send_sem=send_sem.at[d],
                        recv_sem=recv_sem.at[other],
                        device_id=peer,
                        device_id_type=MESH,
                    ),
                )
            )
            copies[-1][0].start()
        return copies

    def to_sibling(i, src, dst):
        copy = pltpu.make_async_remote_copy(
            src_ref=src,
            dst_ref=dst,
            send_sem=part_send.at[i],
            recv_sem=part_recv.at[i],
            device_id=(b, sibling),
            device_id_type=MESH,
        )
        copy.start()
        return copy

    rel_rows = rel_count // 2
    rel_part[0, 0] = rel_acc[0:rel_rows, :]
    rel_part[0, 1] = rel_acc[rel_rows : 2 * rel_rows, :]
    rel_half = to_sibling(0, rel_part.at[0, 1 - core], rel_part.at[1, 0])

    r_own = edges[1:2, pl.ds(pl.multiple_of(first, core_edges), core_edges)]

    def right_columns(start):
        col = lax.broadcasted_iota(jnp.int32, (own_width, core_edges), 0) + start
        pick = jnp.where(col == r_own, 1.0, 0.0).astype(BF16)
        return nt_dot(rrg_hi[...], pick) + nt_dot(rrg_lo[...], pick)

    def left_columns(start):
        return nt_dot(query_s[...], w_s[pl.ds(start, own_width), :])

    right_part[0] = right_columns(sib_start)
    right_half = to_sibling(1, right_part.at[0], right_part.at[1])

    rel_half.wait_recv()
    rb1[j] = rel_part[0, core] + rel_part[1, 0]
    stage1 = exchange(
        rb1, j, inner_peers, [lax.rem(j + d, inner) for d in range(1, inner)], r1_send, r1_recv
    )

    right_own = right_columns(own_start)
    right_half.wait_recv()
    back_send[...] = (right_own + right_part[1]).astype(BF16)
    back = pltpu.make_async_remote_copy(
        src_ref=back_send,
        dst_ref=right_out,
        send_sem=back_ssem,
        recv_sem=back_rsem,
        device_id=(prv, s),
        device_id_type=MESH,
    )
    back.start()

    left_part[0] = left_columns(sib_start)
    left_half = to_sibling(2, left_part.at[0], left_part.at[1])

    for _, incoming in stage1:
        incoming.wait_recv()
    rb2[zi] = jnp.sum(rb1[...], axis=0)
    stage2 = exchange(
        rb2, zi, outer_peers, [lax.rem(zi + d, outer) for d in range(1, outer)], r2_send, r2_recv
    )

    left_own = left_columns(own_start)
    left_half.wait_recv()
    left_stage[...] = left_own + left_part[1]
    left_copy = pltpu.make_async_copy(left_stage, left_out, out_sem.at[0])
    left_copy.start()

    for _, incoming in stage2:
        incoming.wait_recv()
    rb3[...] = jnp.sum(rb2[...], axis=0)
    own_rel = pltpu.make_async_copy(rb3, rel_out.at[core], out_sem.at[1])
    own_rel.start()
    rel_whole = to_sibling(3, rb3, rel_out.at[core])
    back.wait_recv()
    pltpu.make_async_remote_copy(
        src_ref=rb3,
        dst_ref=rel_out.at[1 - core],
        send_sem=part_send.at[3],
        recv_sem=part_recv.at[3],
        device_id=(b, sibling),
        device_id_type=MESH,
    ).wait_recv()

    for copy in fwd + idx_copies + passes:
        copy.wait_send()
    back.wait_send()
    for stage in (stage1, stage2):
        for outgoing, _ in stage:
            outgoing.wait_send()
    for copy in (rel_half, right_half, left_half, rel_whole):
        copy.wait_send()
    left_copy.wait()
    own_rel.wait()


def finish(left_in, right_in, rel_in, left_out, right_out, rel_out, left_v, right_b, right_f, rel_v, sems):
    right_copy = pltpu.make_async_copy(right_in, right_b, sems.at[0])
    right_copy.start()
    rel_copy = pltpu.make_async_copy(rel_in, rel_v, sems.at[1])
    rel_copy.start()
    left_copy = pltpu.make_async_copy(left_in, left_v, sems.at[2])
    left_copy.start()
    right_copy.wait()
    right_f[...] = right_b[...].astype(F32)
    right_done = pltpu.make_async_copy(right_f, right_out, sems.at[3])
    right_done.start()
    left_copy.wait()
    left_done = pltpu.make_async_copy(left_v, left_out, sems.at[5])
    left_done.start()
    rel_copy.wait()
    rel_done = pltpu.make_async_copy(rel_v, rel_out, sems.at[4])
    rel_done.start()
    left_done.wait()
    right_done.wait()
    rel_done.wait()


def solution(mesh):
    n_bucket = mesh.shape["bucket"]
    n_span = mesh.shape["span"]
    inner = math.isqrt(n_bucket)
    outer = n_bucket // inner

    def per_device(
        left_emb,
        right_emb,
        relation_weight,
        left_index,
        right_index,
        relation_index,
        edge_count,
        neg_index,
    ):
        width, part = left_emb.shape
        slots = left_index.shape[2]
        total_edges = 2 * slots
        own = part // n_span
        rel_count = relation_weight.shape[1]
        rel_rows = rel_count // 2
        any_space = pl.BlockSpec(memory_space=pl.ANY)
        dma = pltpu.SemaphoreType.DMA
        left_grad, right_grad, rel_grad = pl.pallas_call(
            functools.partial(kernel, inner),
            out_shape=(
                jax.ShapeDtypeStruct((width, own), F32),
                jax.ShapeDtypeStruct((width, own), BF16),
                jax.ShapeDtypeStruct((2, rel_rows, width), F32),
            ),
            in_specs=[pl.BlockSpec(memory_space=pltpu.HBM)] * 8,
            out_specs=[any_space] * 3,
            scratch_shapes=[
                pltpu.VMEM((width, part), BF16),
                pltpu.VMEM((part, width), BF16),
                pltpu.VMEM((rel_count, width), F32),
                pltpu.VMEM((width, 128), BF16),
                pltpu.VMEM((3, 1, slots), jnp.int32),
                pltpu.VMEM((1, 1), jnp.int32),
                pltpu.VMEM((1, neg_index.shape[1]), jnp.int32),
                pltpu.VMEM((part, 128), F32),
                pltpu.VMEM((n_span, 4, slots), jnp.int32),
                pltpu.VMEM((4, total_edges), jnp.int32),
                pltpu.VMEM((CHUNKS, width, part // CHUNKS), BF16),
                pltpu.VMEM((width, slots), BF16),
                pltpu.VMEM((part, slots), BF16),
                pltpu.VMEM((width, slots), BF16),
                pltpu.VMEM((width, slots), BF16),
                pltpu.VMEM((rel_count, width), F32),
                pltpu.VMEM((width, own), BF16),
                pltpu.VMEM((width, own), F32),
                pltpu.VMEM((width, slots), F32),
                pltpu.VMEM((2, 2, rel_rows, width), F32),
                pltpu.VMEM((2, width, own), F32),
                pltpu.VMEM((2, width, own), F32),
                pltpu.VMEM((inner, rel_rows, width), F32),
                pltpu.VMEM((outer, rel_rows, width), F32),
                pltpu.VMEM((rel_rows, width), F32),
                dma((7,)),
                dma((n_span - 1,)),
                dma((n_span,)),
                dma((CHUNKS // 2,)),
                dma((CHUNKS,)),
                dma((CHUNKS // 2,)),
                dma,
                dma,
                dma((4,)),
                dma((4,)),
                dma((inner,)),
                dma((inner,)),
                dma((outer,)),
                dma((outer,)),
                dma((2,)),
            ],
            compiler_params=pltpu.CompilerParams(
                collective_id=0, has_side_effects=True, vmem_limit_bytes=63 * 1024 * 1024
            ),
        )(
            left_emb,
            right_emb,
            relation_weight.T,
            left_index,
            right_index,
            relation_index,
            edge_count,
            neg_index,
        )
        left_grad, right_grad, rel_grad = pl.pallas_call(
            finish,
            out_shape=(
                jax.ShapeDtypeStruct((width, own), F32),
                jax.ShapeDtypeStruct((width, own), F32),
                jax.ShapeDtypeStruct((rel_count, width), F32),
            ),
            in_specs=[any_space] * 3,
            out_specs=[any_space] * 3,
            scratch_shapes=[
                pltpu.VMEM((width, own), F32),
                pltpu.VMEM((width, own), BF16),
                pltpu.VMEM((width, own), F32),
                pltpu.VMEM((rel_count, width), F32),
                dma((6,)),
            ],
        )(left_grad, right_grad, rel_grad.reshape(rel_count, width))
        return left_grad, right_grad, rel_grad.T

    in_specs = (
        P(None, "bucket"),
        P(None, "bucket"),
        P(),
        P("bucket", "span", None),
        P("bucket", "span", None),
        P("bucket", "span", None),
        P("bucket", "span"),
        P("bucket", None),
    )
    out_specs = (P(None, ("bucket", "span")), P(None, ("bucket", "span")), P())
    return jax.shard_map(
        per_device, mesh=mesh, in_specs=in_specs, out_specs=out_specs, check_vma=False
    )
```

```python
import functools
import math

import jax
import jax.numpy as jnp
from jax import lax
from jax.experimental import pallas as pl
from jax.experimental.pallas import tpu as pltpu
from jax.sharding import PartitionSpec as P

MESH = pl.DeviceIdType.MESH
CHUNKS = 4
TILE = 512
F32 = jnp.float32
BF16 = jnp.bfloat16


def nt_dot(a, b):
    return lax.dot_general(a, b, (((1,), (1,)), ((), ())), preferred_element_type=F32)


def dot(a, b):
    return jnp.dot(a, b, preferred_element_type=F32)


def kernel(
    inner,
    left_hbm,
    right_hbm,
    relw_hbm,
    lidx_hbm,
    ridx_hbm,
    relidx_hbm,
    count_hbm,
    neg_hbm,
    left_out,
    right_out,
    rel_out,
    left,
    left_t,
    relw,
    wcat,
    own_idx,
    own_count,
    neg,
    cnt,
    idx_buf,
    edges,
    rbuf,
    query_s,
    w_s,
    rrg_hi,
    rrg_lo,
    rel_acc,
    back_send,
    left_stage,
    right_rows_s,
    left_rows_s,
    rot_s,
    grad_s,
    pos_s,
    rel_part,
    right_part,
    left_part,
    rb1,
    rb2,
    rb3,
    load_sem,
    idx_send,
    idx_recv,
    fwd_send,
    fwd_recv,
    pass_send,
    back_ssem,
    back_rsem,
    part_send,
    part_recv,
    r1_send,
    r1_recv,
    r2_send,
    r2_recv,
    out_sem,
):
    width, part = left.shape
    half = width // 2
    n_bucket = lax.axis_size("bucket")
    n_span = lax.axis_size("span")
    outer = n_bucket // inner
    b = lax.axis_index("bucket")
    s = lax.axis_index("span")
    count_neg = neg.shape[1]
    total_edges = edges.shape[1]
    slots = own_idx.shape[2]
    own_width = part // n_span
    chunk = part // CHUNKS
    core = lax.rem(s, 2)
    sibling = s + 1 - 2 * core
    nxt = lax.rem(b + 1, n_bucket)
    prv = lax.rem(b + n_bucket - 1, n_bucket)
    j = lax.rem(b, inner)
    zi = lax.div(b, inner)

    barrier = pltpu.get_barrier_semaphore()
    peers = [(nxt, s), (prv, s)]
    span_peers = [(b, lax.rem(s + d, n_span)) for d in range(1, n_span)]
    inner_peers = [(zi * inner + lax.rem(j + d, inner), s) for d in range(1, inner)]
    outer_peers = [(lax.rem(zi + d, outer) * inner + j, s) for d in range(1, outer)]
    peers = outer_peers[::-1] + span_peers + inner_peers + peers
    for peer in peers:
        pl.semaphore_signal(barrier, inc=1, device_id=peer, device_id_type=MESH)
    loads = [
        pltpu.make_async_copy(src, dst, load_sem.at[i])
        for i, (src, dst) in enumerate(
            [
                (lidx_hbm.at[0], own_idx.at[0]),
                (ridx_hbm.at[0], own_idx.at[1]),
                (relidx_hbm.at[0], own_idx.at[2]),
                (count_hbm, own_count),
                (neg_hbm, neg),
                (relw_hbm, relw),
                (left_hbm, left),
            ]
        )
    ]
    for load in loads:
        load.start()

    pl.semaphore_wait(barrier, len(peers))

    fwd = []
    for i in range(CHUNKS // 2):
        k = core * (CHUNKS // 2) + i
        fwd.append(
            pltpu.make_async_remote_copy(
                src_ref=right_hbm.at[:, pl.ds(pl.multiple_of(k * chunk, chunk), chunk)],
                dst_ref=rbuf.at[k],
                send_sem=fwd_send.at[i],
                recv_sem=fwd_recv.at[k],
                device_id=(nxt, s),
                device_id_type=MESH,
            )
        )
        fwd[-1].start()

    for load in loads[:4]:
        load.wait()
    slot = lax.broadcasted_iota(jnp.int32, (1, slots), 1)
    live = slot < own_count[...]
    idx_buf[s, 0:1, :] = jnp.where(live, own_idx[0], -1)
    idx_buf[s, 1:2, :] = own_idx[1]
    idx_buf[s, 2:3, :] = own_idx[2]
    idx_buf[s, 3:4, :] = jnp.zeros((1, slots), jnp.int32)

    idx_copies = []
    for d, peer in enumerate(span_peers):
        idx_copies.append(
            pltpu.make_async_remote_copy(
                src_ref=idx_buf.at[s],
                dst_ref=idx_buf.at[s],
                send_sem=idx_send.at[d],
                recv_sem=idx_recv.at[s],
                device_id=peer,
                device_id_type=MESH,
            )
        )
        idx_copies[-1].start()

    loads[4].wait()
    for k in range(part // 128):
        col = lax.broadcasted_iota(jnp.int32, (128, count_neg), 0) + k * 128
        hits = jnp.where(col == neg[...], 1.0, 0.0).astype(F32)
        times = jnp.sum(hits, axis=1, keepdims=True) * (1.0 / count_neg)
        cnt[k * 128 : (k + 1) * 128, :] = jnp.broadcast_to(times, (128, 128))

    loads[5].wait()
    rel_count = relw.shape[0]
    w0 = relw[...]
    w_hi = w0.astype(BF16).astype(F32)
    w_mid = (w0 - w_hi).astype(BF16).astype(F32)
    w_lo = w0 - w_hi - w_mid
    blank = jnp.zeros((128 - 3 * rel_count, width), F32)
    wcat[...] = jnp.concatenate([w_hi, w_mid, w_lo, blank], axis=0).T.astype(BF16)

    loads[6].wait()
    for k in range(part // 128):
        block = left[:, k * 128 : (k + 1) * 128].astype(F32)
        left_t[k * 128 : (k + 1) * 128, :] = block.T.astype(BF16)

    for d in range(1, n_span):
        c = lax.rem(s + d, n_span)
        pltpu.make_async_remote_copy(
            src_ref=idx_buf.at[c],
            dst_ref=idx_buf.at[c],
            send_sem=idx_send.at[d - 1],
            recv_sem=idx_recv.at[c],
            device_id=(b, c),
            device_id_type=MESH,
        ).wait_recv()
    lefts = jnp.concatenate([idx_buf[c, 0:1, :] for c in range(n_span)], axis=0)
    rights = jnp.concatenate([idx_buf[c, 1:2, :] for c in range(n_span)], axis=0)
    kinds = jnp.concatenate([idx_buf[c, 2:3, :] for c in range(n_span)], axis=0)
    sizes = jnp.sum(jnp.where(lefts >= 0, 1.0, 0.0).astype(F32), axis=1, keepdims=True)
    sizes = sizes.astype(jnp.int32)
    begins = [jnp.zeros((1, 1), jnp.int32)]
    for c in range(n_span - 1):
        begins.append(begins[-1] + sizes[c : c + 1])
    start = jnp.concatenate(begins, axis=0)
    bits = (part - 1).bit_length()
    packed = jnp.maximum(lefts, 0) + (rights << bits) + (kinds << (2 * bits))
    packed = jnp.concatenate(
        [packed, jnp.zeros((n_span, total_edges - slots), jnp.int32)], axis=1
    )
    for bit in range((total_edges - 1).bit_length()):
        moved = pltpu.roll(packed, 1 << bit, 1)
        on = jnp.broadcast_to(start & (1 << bit), (n_span, total_edges)) != 0
        packed = jnp.where(on, moved, packed)
    rank = lax.broadcasted_iota(jnp.int32, (n_span, total_edges), 1)
    packed = jnp.where((rank >= start) & (rank < start + sizes), packed, 0)
    line = packed[0:1]
    for c in range(1, n_span):
        line = line + packed[c : c + 1]
    edges[0:1, :] = line & (part - 1)
    edges[1:2, :] = (line >> bits) & (part - 1)
    edges[2:3, :] = line >> (2 * bits)

    core_edges = total_edges // 2
    first = core * core_edges

    for t in range(core_edges // TILE):
        at = slice(t * TILE, (t + 1) * TILE)
        edge_at = pl.ds(pl.multiple_of(first + t * TILE, TILE), TILE)
        kind = lax.broadcasted_iota(jnp.int32, (128, TILE), 0)
        pick_rel = jnp.where((kind & (rel_count - 1)) == edges[2:3, edge_at], 1.0, 0.0).astype(BF16)
        rot_s[:, at] = dot(wcat[...], pick_rel)
        col = lax.broadcasted_iota(jnp.int32, (part, TILE), 0)
        pick = jnp.where(col == edges[0:1, edge_at], 1.0, 0.0).astype(BF16)
        left_rows_s[:, at] = dot(left[...], pick)

    def gather(k, fresh):
        for t in range(core_edges // TILE):
            r_row = edges[1:2, pl.ds(pl.multiple_of(first + t * TILE, TILE), TILE)]
            col = lax.broadcasted_iota(jnp.int32, (chunk, TILE), 0) + k * chunk
            pick = jnp.where(col == r_row, 1.0, 0.0).astype(BF16)
            found = dot(rbuf[k], pick)
            at = slice(t * TILE, (t + 1) * TILE)
            right_rows_s[:, at] = found if fresh else right_rows_s[:, at] + found

    passes = []
    for i in range(CHUNKS // 2):
        k = core * (CHUNKS // 2) + i
        fwd[i].wait_recv()
        passes.append(
            pltpu.make_async_remote_copy(
                src_ref=rbuf.at[k],
                dst_ref=rbuf.at[k],
                send_sem=pass_send.at[i],
                recv_sem=fwd_recv.at[k],
                device_id=(b, sibling),
                device_id_type=MESH,
            )
        )
        passes[-1].start()
        gather(k, i == 0)
    for i in range(CHUNKS // 2):
        k = (1 - core) * (CHUNKS // 2) + i
        pltpu.make_async_remote_copy(
            src_ref=rbuf.at[k],
            dst_ref=rbuf.at[k],
            send_sem=pass_send.at[i],
            recv_sem=fwd_recv.at[k],
            device_id=(b, sibling),
            device_id_type=MESH,
        ).wait_recv()
        gather(k, False)

    rel_acc[...] = jnp.zeros_like(rel_acc)
    own_start = pl.multiple_of(s * own_width, own_width)
    sib_start = pl.multiple_of(sibling * own_width, own_width)

    def tile_step(t):
        at = slice(t * TILE, (t + 1) * TILE)
        edge_at = pl.ds(pl.multiple_of(first + t * TILE, TILE), TILE)
        t_row = edges[2:3, edge_at]
        right_rows = right_rows_s[:, at]
        left_rows = left_rows_s[:, at]
        rot = rot_s[:, at]
        w_re, w_im = rot[:half], rot[half:]
        r_re, r_im = right_rows[:half], right_rows[half:]
        query = jnp.concatenate(
            [w_re * r_re + w_im * r_im, w_re * r_im - w_im * r_re], axis=0
        ).astype(BF16)
        query_s[:, at] = query
        positive = jnp.sum(left_rows * query.astype(F32), axis=0, keepdims=True)
        pos_weight = -1.0 / (1.0 + jnp.exp(positive))
        pos_s[:, at] = pos_weight
        scores = dot(left_t[...], query)
        times = jnp.concatenate([cnt[...]] * (TILE // 128), axis=1)
        weight = (times * pl.reciprocal(1.0 + jnp.exp(-scores), approx=True)).astype(BF16)
        w_s[:, at] = weight
        grad = dot(left[...], weight) + left_rows * pos_weight
        grad_s[:, at] = grad
        a, c = grad[:half], grad[half:]
        turn = jnp.concatenate([a * r_re + c * r_im, a * r_im - c * r_re], axis=0).astype(BF16)
        own_kind = lax.broadcasted_iota(jnp.int32, (rel_count, TILE), 0)
        pick_own = jnp.where(own_kind == t_row, 1.0, 0.0).astype(BF16)
        rel_acc[...] += nt_dot(pick_own, turn)

    for t in range(core_edges // TILE):
        tile_step(t)

    def exchange(buf, me, peers, slots_of, send_sem, recv_sem):
        copies = []
        for d, (peer, other) in enumerate(zip(peers, slots_of)):
            copies.append(
                (
                    pltpu.make_async_remote_copy(
                        src_ref=buf.at[me],
                        dst_ref=buf.at[me],
                        send_sem=send_sem.at[d],
                        recv_sem=recv_sem.at[me],
                        device_id=peer,
                        device_id_type=MESH,
                    ),
                    pltpu.make_async_remote_copy(
                        src_ref=buf.at[other],
                        dst_ref=buf.at[other],
                        send_sem=send_sem.at[d],
                        recv_sem=recv_sem.at[other],
                        device_id=peer,
                        device_id_type=MESH,
                    ),
                )
            )
            copies[-1][0].start()
        return copies

    def to_sibling(i, src, dst):
        copy = pltpu.make_async_remote_copy(
            src_ref=src,
            dst_ref=dst,
            send_sem=part_send.at[i],
            recv_sem=part_recv.at[i],
            device_id=(b, sibling),
            device_id_type=MESH,
        )
        copy.start()
        return copy

    rel_rows = rel_count // 2
    rel_part[0, 0] = rel_acc[0:rel_rows, :]
    rel_part[0, 1] = rel_acc[rel_rows : 2 * rel_rows, :]
    rel_half = to_sibling(0, rel_part.at[0, 1 - core], rel_part.at[1, 0])

    for t in range(core_edges // TILE):
        at = slice(t * TILE, (t + 1) * TILE)
        a, c = grad_s[:half, at], grad_s[half:, at]
        w_re, w_im = rot_s[:half, at], rot_s[half:, at]
        rows = jnp.concatenate([a * w_re - c * w_im, a * w_im + c * w_re], axis=0)
        hi = rows.astype(BF16)
        rrg_hi[:, at] = hi
        rrg_lo[:, at] = (rows - hi.astype(F32)).astype(BF16)
    l_own = edges[0:1, pl.ds(pl.multiple_of(first, core_edges), core_edges)]
    r_own = edges[1:2, pl.ds(pl.multiple_of(first, core_edges), core_edges)]

    def right_columns(start):
        col = lax.broadcasted_iota(jnp.int32, (own_width, core_edges), 0) + start
        pick = jnp.where(col == r_own, 1.0, 0.0).astype(BF16)
        return nt_dot(rrg_hi[...], pick) + nt_dot(rrg_lo[...], pick)

    def left_columns(start):
        col = lax.broadcasted_iota(jnp.int32, (own_width, core_edges), 0) + start
        pick = jnp.where(col == l_own, 1.0, 0.0).astype(BF16)
        scaled = query_s[...].astype(F32) * pos_s[...]
        hi = scaled.astype(BF16)
        lo = (scaled - hi.astype(F32)).astype(BF16)
        sums = nt_dot(query_s[...], w_s[pl.ds(start, own_width), :])
        return sums + nt_dot(hi, pick) + nt_dot(lo, pick)

    right_part[0] = right_columns(sib_start)
    right_half = to_sibling(1, right_part.at[0], right_part.at[1])

    rel_half.wait_recv()
    rb1[j] = rel_part[0, core] + rel_part[1, 0]
    stage1 = exchange(
        rb1, j, inner_peers, [lax.rem(j + d, inner) for d in range(1, inner)], r1_send, r1_recv
    )

    right_own = right_columns(own_start)
    right_half.wait_recv()
    back_send[...] = (right_own + right_part[1]).astype(BF16)
    back = pltpu.make_async_remote_copy(
        src_ref=back_send,
        dst_ref=right_out,
        send_sem=back_ssem,
        recv_sem=back_rsem,
        device_id=(prv, s),
        device_id_type=MESH,
    )
    back.start()

    left_part[0] = left_columns(sib_start)
    left_half = to_sibling(2, left_part.at[0], left_part.at[1])

    for _, incoming in stage1:
        incoming.wait_recv()
    rb2[zi] = jnp.sum(rb1[...], axis=0)
    stage2 = exchange(
        rb2, zi, outer_peers, [lax.rem(zi + d, outer) for d in range(1, outer)], r2_send, r2_recv
    )

    left_own = left_columns(own_start)
    left_half.wait_recv()
    left_stage[...] = left_own + left_part[1]
    left_copy = pltpu.make_async_copy(left_stage, left_out, out_sem.at[0])
    left_copy.start()

    for _, incoming in stage2:
        incoming.wait_recv()
    rb3[...] = jnp.sum(rb2[...], axis=0)
    own_rel = pltpu.make_async_copy(rb3, rel_out.at[core], out_sem.at[1])
    own_rel.start()
    rel_whole = to_sibling(3, rb3, rel_out.at[core])
    back.wait_recv()
    pltpu.make_async_remote_copy(
        src_ref=rb3,
        dst_ref=rel_out.at[1 - core],
        send_sem=part_send.at[3],
        recv_sem=part_recv.at[3],
        device_id=(b, sibling),
        device_id_type=MESH,
    ).wait_recv()

    for copy in fwd + idx_copies + passes:
        copy.wait_send()
    back.wait_send()
    for stage in (stage1, stage2):
        for outgoing, _ in stage:
            outgoing.wait_send()
    for copy in (rel_half, right_half, left_half, rel_whole):
        copy.wait_send()
    left_copy.wait()
    own_rel.wait()


def finish(left_in, right_in, rel_in, left_out, right_out, rel_out, left_v, right_b, right_f, rel_v, sems):
    right_copy = pltpu.make_async_copy(right_in, right_b, sems.at[0])
    right_copy.start()
    rel_copy = pltpu.make_async_copy(rel_in, rel_v, sems.at[1])
    rel_copy.start()
    left_copy = pltpu.make_async_copy(left_in, left_v, sems.at[2])
    left_copy.start()
    right_copy.wait()
    right_f[...] = right_b[...].astype(F32)
    right_done = pltpu.make_async_copy(right_f, right_out, sems.at[3])
    right_done.start()
    left_copy.wait()
    left_done = pltpu.make_async_copy(left_v, left_out, sems.at[5])
    left_done.start()
    rel_copy.wait()
    rel_done = pltpu.make_async_copy(rel_v, rel_out, sems.at[4])
    rel_done.start()
    left_done.wait()
    right_done.wait()
    rel_done.wait()


def solution(mesh):
    n_bucket = mesh.shape["bucket"]
    n_span = mesh.shape["span"]
    inner = math.isqrt(n_bucket)
    outer = n_bucket // inner

    def per_device(
        left_emb,
        right_emb,
        relation_weight,
        left_index,
        right_index,
        relation_index,
        edge_count,
        neg_index,
    ):
        width, part = left_emb.shape
        slots = left_index.shape[2]
        total_edges = 2 * slots
        own = part // n_span
        rel_count = relation_weight.shape[1]
        rel_rows = rel_count // 2
        any_space = pl.BlockSpec(memory_space=pl.ANY)
        dma = pltpu.SemaphoreType.DMA
        left_grad, right_grad, rel_grad = pl.pallas_call(
            functools.partial(kernel, inner),
            out_shape=(
                jax.ShapeDtypeStruct((width, own), F32),
                jax.ShapeDtypeStruct((width, own), BF16),
                jax.ShapeDtypeStruct((2, rel_rows, width), F32),
            ),
            in_specs=[pl.BlockSpec(memory_space=pltpu.HBM)] * 8,
            out_specs=[any_space] * 3,
            scratch_shapes=[
                pltpu.VMEM((width, part), BF16),
                pltpu.VMEM((part, width), BF16),
                pltpu.VMEM((rel_count, width), F32),
                pltpu.VMEM((width, 128), BF16),
                pltpu.VMEM((3, 1, slots), jnp.int32),
                pltpu.VMEM((1, 1), jnp.int32),
                pltpu.VMEM((1, neg_index.shape[1]), jnp.int32),
                pltpu.VMEM((part, 128), F32),
                pltpu.VMEM((n_span, 4, slots), jnp.int32),
                pltpu.VMEM((3, total_edges), jnp.int32),
                pltpu.VMEM((CHUNKS, width, part // CHUNKS), BF16),
                pltpu.VMEM((width, slots), BF16),
                pltpu.VMEM((part, slots), BF16),
                pltpu.VMEM((width, slots), BF16),
                pltpu.VMEM((width, slots), BF16),
                pltpu.VMEM((rel_count, width), F32),
                pltpu.VMEM((width, own), BF16),
                pltpu.VMEM((width, own), F32),
                pltpu.VMEM((width, slots), F32),
                pltpu.VMEM((width, slots), F32),
                pltpu.VMEM((width, slots), F32),
                pltpu.VMEM((width, slots), F32),
                pltpu.VMEM((1, slots), F32),
                pltpu.VMEM((2, 2, rel_rows, width), F32),
                pltpu.VMEM((2, width, own), F32),
                pltpu.VMEM((2, width, own), F32),
                pltpu.VMEM((inner, rel_rows, width), F32),
                pltpu.VMEM((outer, rel_rows, width), F32),
                pltpu.VMEM((rel_rows, width), F32),
                dma((7,)),
                dma((n_span - 1,)),
                dma((n_span,)),
                dma((CHUNKS // 2,)),
                dma((CHUNKS,)),
                dma((CHUNKS // 2,)),
                dma,
                dma,
                dma((4,)),
                dma((4,)),
                dma((inner,)),
                dma((inner,)),
                dma((outer,)),
                dma((outer,)),
                dma((2,)),
            ],
            compiler_params=pltpu.CompilerParams(
                collective_id=0, has_side_effects=True, vmem_limit_bytes=63 * 1024 * 1024
            ),
        )(
            left_emb,
            right_emb,
            relation_weight.T,
            left_index,
            right_index,
            relation_index,
            edge_count,
            neg_index,
        )
        left_grad, right_grad, rel_grad = pl.pallas_call(
            finish,
            out_shape=(
                jax.ShapeDtypeStruct((width, own), F32),
                jax.ShapeDtypeStruct((width, own), F32),
                jax.ShapeDtypeStruct((rel_count, width), F32),
            ),
            in_specs=[any_space] * 3,
            out_specs=[any_space] * 3,
            scratch_shapes=[
                pltpu.VMEM((width, own), F32),
                pltpu.VMEM((width, own), BF16),
                pltpu.VMEM((width, own), F32),
                pltpu.VMEM((rel_count, width), F32),
                dma((6,)),
            ],
        )(left_grad, right_grad, rel_grad.reshape(rel_count, width))
        return left_grad, right_grad, rel_grad.T

    in_specs = (
        P(None, "bucket"),
        P(None, "bucket"),
        P(),
        P("bucket", "span", None),
        P("bucket", "span", None),
        P("bucket", "span", None),
        P("bucket", "span"),
        P("bucket", None),
    )
    out_specs = (P(None, ("bucket", "span")), P(None, ("bucket", "span")), P())
    return jax.shard_map(
        per_device, mesh=mesh, in_specs=in_specs, out_specs=out_specs, check_vma=False
    )
```

```python
import functools
import math

import jax
import jax.numpy as jnp
from jax import lax
from jax.experimental import pallas as pl
from jax.experimental.pallas import tpu as pltpu
from jax.sharding import PartitionSpec as P

MESH = pl.DeviceIdType.MESH
CHUNKS = 4
TILE = 512
F32 = jnp.float32
BF16 = jnp.bfloat16


def nt_dot(a, b):
    return lax.dot_general(a, b, (((1,), (1,)), ((), ())), preferred_element_type=F32)


def dot(a, b):
    return jnp.dot(a, b, preferred_element_type=F32)


def kernel(
    inner,
    left_hbm,
    right_hbm,
    relw_hbm,
    lidx_hbm,
    ridx_hbm,
    relidx_hbm,
    count_hbm,
    neg_hbm,
    left_out,
    right_out,
    rel_out,
    left,
    left_t,
    relw,
    wcat,
    own_idx,
    own_count,
    neg,
    cnt,
    idx_buf,
    edges,
    rbuf,
    query_s,
    w_s,
    rrg_hi,
    rel_acc,
    back_send,
    left_stage,
    right_rows_s,
    left_rows_s,
    rot_s,
    grad_s,
    pos_s,
    rel_part,
    right_part,
    left_part,
    rb1,
    rb2,
    rb3,
    load_sem,
    idx_send,
    idx_recv,
    fwd_send,
    fwd_recv,
    pass_send,
    back_ssem,
    back_rsem,
    part_send,
    part_recv,
    r1_send,
    r1_recv,
    r2_send,
    r2_recv,
    out_sem,
):
    width, part = left.shape
    half = width // 2
    n_bucket = lax.axis_size("bucket")
    n_span = lax.axis_size("span")
    outer = n_bucket // inner
    b = lax.axis_index("bucket")
    s = lax.axis_index("span")
    count_neg = neg.shape[1]
    total_edges = edges.shape[1]
    slots = own_idx.shape[2]
    own_width = part // n_span
    chunk = part // CHUNKS
    core = lax.rem(s, 2)
    sibling = s + 1 - 2 * core
    nxt = lax.rem(b + 1, n_bucket)
    prv = lax.rem(b + n_bucket - 1, n_bucket)
    j = lax.rem(b, inner)
    zi = lax.div(b, inner)

    barrier = pltpu.get_barrier_semaphore()
    peers = [(nxt, s), (prv, s)]
    span_peers = [(b, lax.rem(s + d, n_span)) for d in range(1, n_span)]
    inner_peers = [(zi * inner + lax.rem(j + d, inner), s) for d in range(1, inner)]
    outer_peers = [(lax.rem(zi + d, outer) * inner + j, s) for d in range(1, outer)]
    peers = outer_peers[::-1] + span_peers + inner_peers + peers
    for peer in peers:
        pl.semaphore_signal(barrier, inc=1, device_id=peer, device_id_type=MESH)
    loads = [
        pltpu.make_async_copy(src, dst, load_sem.at[i])
        for i, (src, dst) in enumerate(
            [
                (lidx_hbm.at[0], own_idx.at[0]),
                (ridx_hbm.at[0], own_idx.at[1]),
                (relidx_hbm.at[0], own_idx.at[2]),
                (count_hbm, own_count),
                (neg_hbm, neg),
                (relw_hbm, relw),
                (left_hbm, left),
            ]
        )
    ]
    for load in loads:
        load.start()

    pl.semaphore_wait(barrier, len(peers))

    fwd = []
    for i in range(CHUNKS // 2):
        k = core * (CHUNKS // 2) + i
        fwd.append(
            pltpu.make_async_remote_copy(
                src_ref=right_hbm.at[:, pl.ds(pl.multiple_of(k * chunk, chunk), chunk)],
                dst_ref=rbuf.at[k],
                send_sem=fwd_send.at[i],
                recv_sem=fwd_recv.at[k],
                device_id=(nxt, s),
                device_id_type=MESH,
            )
        )
        fwd[-1].start()

    for load in loads[:4]:
        load.wait()
    slot = lax.broadcasted_iota(jnp.int32, (1, slots), 1)
    live = slot < own_count[...]
    idx_buf[s, 0:1, :] = jnp.where(live, own_idx[0], -1)
    idx_buf[s, 1:2, :] = own_idx[1]
    idx_buf[s, 2:3, :] = own_idx[2]
    idx_buf[s, 3:4, :] = jnp.zeros((1, slots), jnp.int32)

    idx_copies = []
    for d, peer in enumerate(span_peers):
        idx_copies.append(
            pltpu.make_async_remote_copy(
                src_ref=idx_buf.at[s],
                dst_ref=idx_buf.at[s],
                send_sem=idx_send.at[d],
                recv_sem=idx_recv.at[s],
                device_id=peer,
                device_id_type=MESH,
            )
        )
        idx_copies[-1].start()

    loads[4].wait()
    for k in range(part // 128):
        col = lax.broadcasted_iota(jnp.int32, (128, count_neg), 0) + k * 128
        hits = jnp.where(col == neg[...], 1.0, 0.0).astype(F32)
        times = jnp.sum(hits, axis=1, keepdims=True) * (1.0 / count_neg)
        cnt[k * 128 : (k + 1) * 128, :] = jnp.broadcast_to(times, (128, 128))

    loads[5].wait()
    rel_count = relw.shape[0]
    w0 = relw[...]
    w_hi = w0.astype(BF16).astype(F32)
    w_mid = (w0 - w_hi).astype(BF16).astype(F32)
    w_lo = w0 - w_hi - w_mid
    blank = jnp.zeros((128 - 3 * rel_count, width), F32)
    wcat[...] = jnp.concatenate([w_hi, w_mid, w_lo, blank], axis=0).T.astype(BF16)

    loads[6].wait()
    for k in range(part // 128):
        block = left[:, k * 128 : (k + 1) * 128].astype(F32)
        left_t[k * 128 : (k + 1) * 128, :] = block.T.astype(BF16)

    for d in range(1, n_span):
        c = lax.rem(s + d, n_span)
        pltpu.make_async_remote_copy(
            src_ref=idx_buf.at[c],
            dst_ref=idx_buf.at[c],
            send_sem=idx_send.at[d - 1],
            recv_sem=idx_recv.at[c],
            device_id=(b, c),
            device_id_type=MESH,
        ).wait_recv()
    lefts = jnp.concatenate([idx_buf[c, 0:1, :] for c in range(n_span)], axis=0)
    rights = jnp.concatenate([idx_buf[c, 1:2, :] for c in range(n_span)], axis=0)
    kinds = jnp.concatenate([idx_buf[c, 2:3, :] for c in range(n_span)], axis=0)
    sizes = jnp.sum(jnp.where(lefts >= 0, 1.0, 0.0).astype(F32), axis=1, keepdims=True)
    sizes = sizes.astype(jnp.int32)
    begins = [jnp.zeros((1, 1), jnp.int32)]
    for c in range(n_span - 1):
        begins.append(begins[-1] + sizes[c : c + 1])
    start = jnp.concatenate(begins, axis=0)
    bits = (part - 1).bit_length()
    packed = jnp.maximum(lefts, 0) + (rights << bits) + (kinds << (2 * bits))
    packed = jnp.concatenate(
        [packed, jnp.zeros((n_span, total_edges - slots), jnp.int32)], axis=1
    )
    for bit in range((total_edges - 1).bit_length()):
        moved = pltpu.roll(packed, 1 << bit, 1)
        on = jnp.broadcast_to(start & (1 << bit), (n_span, total_edges)) != 0
        packed = jnp.where(on, moved, packed)
    rank = lax.broadcasted_iota(jnp.int32, (n_span, total_edges), 1)
    packed = jnp.where((rank >= start) & (rank < start + sizes), packed, 0)
    line = packed[0:1]
    for c in range(1, n_span):
        line = line + packed[c : c + 1]
    edges[0:1, :] = line & (part - 1)
    edges[1:2, :] = (line >> bits) & (part - 1)
    edges[2:3, :] = line >> (2 * bits)

    core_edges = total_edges // 2
    first = core * core_edges

    for t in range(core_edges // TILE):
        at = slice(t * TILE, (t + 1) * TILE)
        edge_at = pl.ds(pl.multiple_of(first + t * TILE, TILE), TILE)
        kind = lax.broadcasted_iota(jnp.int32, (128, TILE), 0)
        pick_rel = jnp.where((kind & (rel_count - 1)) == edges[2:3, edge_at], 1.0, 0.0).astype(BF16)
        rot_s[:, at] = dot(wcat[...], pick_rel)
        col = lax.broadcasted_iota(jnp.int32, (part, TILE), 0)
        pick = jnp.where(col == edges[0:1, edge_at], 1.0, 0.0).astype(BF16)
        left_rows_s[:, at] = dot(left[...], pick)

    def gather(k, fresh):
        for t in range(core_edges // TILE):
            r_row = edges[1:2, pl.ds(pl.multiple_of(first + t * TILE, TILE), TILE)]
            col = lax.broadcasted_iota(jnp.int32, (chunk, TILE), 0) + k * chunk
            pick = jnp.where(col == r_row, 1.0, 0.0).astype(BF16)
            found = dot(rbuf[k], pick)
            at = slice(t * TILE, (t + 1) * TILE)
            right_rows_s[:, at] = found if fresh else right_rows_s[:, at] + found

    passes = []
    for i in range(CHUNKS // 2):
        k = core * (CHUNKS // 2) + i
        fwd[i].wait_recv()
        passes.append(
            pltpu.make_async_remote_copy(
                src_ref=rbuf.at[k],
                dst_ref=rbuf.at[k],
                send_sem=pass_send.at[i],
                recv_sem=fwd_recv.at[k],
                device_id=(b, sibling),
                device_id_type=MESH,
            )
        )
        passes[-1].start()
        gather(k, i == 0)
    for i in range(CHUNKS // 2):
        k = (1 - core) * (CHUNKS // 2) + i
        pltpu.make_async_remote_copy(
            src_ref=rbuf.at[k],
            dst_ref=rbuf.at[k],
            send_sem=pass_send.at[i],
            recv_sem=fwd_recv.at[k],
            device_id=(b, sibling),
            device_id_type=MESH,
        ).wait_recv()
        gather(k, False)

    rel_acc[...] = jnp.zeros_like(rel_acc)
    own_start = pl.multiple_of(s * own_width, own_width)
    sib_start = pl.multiple_of(sibling * own_width, own_width)

    def tile_step(t):
        at = slice(t * TILE, (t + 1) * TILE)
        edge_at = pl.ds(pl.multiple_of(first + t * TILE, TILE), TILE)
        t_row = edges[2:3, edge_at]
        right_rows = right_rows_s[:, at]
        left_rows = left_rows_s[:, at]
        rot = rot_s[:, at]
        w_re, w_im = rot[:half], rot[half:]
        r_re, r_im = right_rows[:half], right_rows[half:]
        query = jnp.concatenate(
            [w_re * r_re + w_im * r_im, w_re * r_im - w_im * r_re], axis=0
        ).astype(BF16)
        query_s[:, at] = query
        positive = jnp.sum(left_rows * query.astype(F32), axis=0, keepdims=True)
        pos_weight = -1.0 / (1.0 + jnp.exp(positive))
        pos_s[:, at] = pos_weight
        scores = dot(left_t[...], query)
        times = jnp.concatenate([cnt[...]] * (TILE // 128), axis=1)
        weight = (times * pl.reciprocal(1.0 + jnp.exp(-scores), approx=True)).astype(BF16)
        w_s[:, at] = weight
        grad = dot(left[...], weight) + left_rows * pos_weight
        grad_s[:, at] = grad
        a, c = grad[:half], grad[half:]
        turn = jnp.concatenate([a * r_re + c * r_im, a * r_im - c * r_re], axis=0).astype(BF16)
        own_kind = lax.broadcasted_iota(jnp.int32, (rel_count, TILE), 0)
        pick_own = jnp.where(own_kind == t_row, 1.0, 0.0).astype(BF16)
        rel_acc[...] += nt_dot(pick_own, turn)

    for t in range(core_edges // TILE):
        tile_step(t)

    def exchange(buf, me, peers, slots_of, send_sem, recv_sem):
        copies = []
        for d, (peer, other) in enumerate(zip(peers, slots_of)):
            copies.append(
                (
                    pltpu.make_async_remote_copy(
                        src_ref=buf.at[me],
                        dst_ref=buf.at[me],
                        send_sem=send_sem.at[d],
                        recv_sem=recv_sem.at[me],
                        device_id=peer,
                        device_id_type=MESH,
                    ),
                    pltpu.make_async_remote_copy(
                        src_ref=buf.at[other],
                        dst_ref=buf.at[other],
                        send_sem=send_sem.at[d],
                        recv_sem=recv_sem.at[other],
                        device_id=peer,
                        device_id_type=MESH,
                    ),
                )
            )
            copies[-1][0].start()
        return copies

    def to_sibling(i, src, dst):
        copy = pltpu.make_async_remote_copy(
            src_ref=src,
            dst_ref=dst,
            send_sem=part_send.at[i],
            recv_sem=part_recv.at[i],
            device_id=(b, sibling),
            device_id_type=MESH,
        )
        copy.start()
        return copy

    rel_rows = rel_count // 2
    rel_part[0, 0] = rel_acc[0:rel_rows, :]
    rel_part[0, 1] = rel_acc[rel_rows : 2 * rel_rows, :]
    rel_half = to_sibling(0, rel_part.at[0, 1 - core], rel_part.at[1, 0])

    for t in range(core_edges // TILE):
        at = slice(t * TILE, (t + 1) * TILE)
        a, c = grad_s[:half, at], grad_s[half:, at]
        w_re, w_im = rot_s[:half, at], rot_s[half:, at]
        rows = jnp.concatenate([a * w_re - c * w_im, a * w_im + c * w_re], axis=0)
        rrg_hi[:, at] = rows.astype(BF16)
    l_own = edges[0:1, pl.ds(pl.multiple_of(first, core_edges), core_edges)]
    r_own = edges[1:2, pl.ds(pl.multiple_of(first, core_edges), core_edges)]

    def right_columns(start):
        col = lax.broadcasted_iota(jnp.int32, (own_width, core_edges), 0) + start
        pick = jnp.where(col == r_own, 1.0, 0.0).astype(BF16)
        return nt_dot(rrg_hi[...], pick)

    def left_columns(start):
        col = lax.broadcasted_iota(jnp.int32, (own_width, core_edges), 0) + start
        pick = jnp.where(col == l_own, 1.0, 0.0).astype(BF16)
        scaled = query_s[...].astype(F32) * pos_s[...]
        hi = scaled.astype(BF16)
        lo = (scaled - hi.astype(F32)).astype(BF16)
        sums = nt_dot(query_s[...], w_s[pl.ds(start, own_width), :])
        return sums + nt_dot(hi, pick) + nt_dot(lo, pick)

    right_part[0] = right_columns(sib_start)
    right_half = to_sibling(1, right_part.at[0], right_part.at[1])

    rel_half.wait_recv()
    rb1[j] = rel_part[0, core] + rel_part[1, 0]
    stage1 = exchange(
        rb1, j, inner_peers, [lax.rem(j + d, inner) for d in range(1, inner)], r1_send, r1_recv
    )

    right_own = right_columns(own_start)
    right_half.wait_recv()
    back_send[...] = (right_own + right_part[1]).astype(BF16)
    back = pltpu.make_async_remote_copy(
        src_ref=back_send,
        dst_ref=right_out,
        send_sem=back_ssem,
        recv_sem=back_rsem,
        device_id=(prv, s),
        device_id_type=MESH,
    )
    back.start()

    left_part[0] = left_columns(sib_start)
    left_half = to_sibling(2, left_part.at[0], left_part.at[1])

    for _, incoming in stage1:
        incoming.wait_recv()
    plane = jnp.sum(rb1[...], axis=0)
    blank = jnp.zeros((rel_rows, 512 - width), F32)
    lower = jnp.concatenate([plane[:, 256:], blank], axis=1)
    rb2[zi] = jnp.concatenate([plane[:, :256], lower], axis=0).astype(BF16)
    stage2 = exchange(
        rb2, zi, outer_peers, [lax.rem(zi + d, outer) for d in range(1, outer)], r2_send, r2_recv
    )

    left_own = left_columns(own_start)
    left_half.wait_recv()
    left_stage[...] = left_own + left_part[1]
    left_copy = pltpu.make_async_copy(left_stage, left_out, out_sem.at[0])
    left_copy.start()

    for _, incoming in stage2:
        incoming.wait_recv()
    whole = jnp.sum(rb2[...].astype(F32), axis=0)
    rb3[:, :256] = whole[:rel_rows]
    rb3[:, 256:] = whole[rel_rows:, : width - 256]
    own_rel = pltpu.make_async_copy(rb3, rel_out.at[core], out_sem.at[1])
    own_rel.start()
    rel_whole = to_sibling(3, rb3, rel_out.at[core])
    back.wait_recv()
    pltpu.make_async_remote_copy(
        src_ref=rb3,
        dst_ref=rel_out.at[1 - core],
        send_sem=part_send.at[3],
        recv_sem=part_recv.at[3],
        device_id=(b, sibling),
        device_id_type=MESH,
    ).wait_recv()

    for copy in fwd + idx_copies + passes:
        copy.wait_send()
    back.wait_send()
    for stage in (stage1, stage2):
        for outgoing, _ in stage:
            outgoing.wait_send()
    for copy in (rel_half, right_half, left_half, rel_whole):
        copy.wait_send()
    left_copy.wait()
    own_rel.wait()


def finish(left_in, right_in, rel_in, left_out, right_out, rel_out, left_v, right_b, right_f, rel_v, sems):
    right_copy = pltpu.make_async_copy(right_in, right_b, sems.at[0])
    right_copy.start()
    rel_copy = pltpu.make_async_copy(rel_in, rel_v, sems.at[1])
    rel_copy.start()
    left_copy = pltpu.make_async_copy(left_in, left_v, sems.at[2])
    left_copy.start()
    right_copy.wait()
    right_f[...] = right_b[...].astype(F32)
    right_done = pltpu.make_async_copy(right_f, right_out, sems.at[3])
    right_done.start()
    left_copy.wait()
    left_done = pltpu.make_async_copy(left_v, left_out, sems.at[5])
    left_done.start()
    rel_copy.wait()
    rel_done = pltpu.make_async_copy(rel_v, rel_out, sems.at[4])
    rel_done.start()
    left_done.wait()
    right_done.wait()
    rel_done.wait()


def solution(mesh):
    n_bucket = mesh.shape["bucket"]
    n_span = mesh.shape["span"]
    inner = math.isqrt(n_bucket)
    outer = n_bucket // inner

    def per_device(
        left_emb,
        right_emb,
        relation_weight,
        left_index,
        right_index,
        relation_index,
        edge_count,
        neg_index,
    ):
        width, part = left_emb.shape
        slots = left_index.shape[2]
        total_edges = 2 * slots
        own = part // n_span
        rel_count = relation_weight.shape[1]
        rel_rows = rel_count // 2
        any_space = pl.BlockSpec(memory_space=pl.ANY)
        dma = pltpu.SemaphoreType.DMA
        left_grad, right_grad, rel_grad = pl.pallas_call(
            functools.partial(kernel, inner),
            out_shape=(
                jax.ShapeDtypeStruct((width, own), F32),
                jax.ShapeDtypeStruct((width, own), BF16),
                jax.ShapeDtypeStruct((2, rel_rows, width), F32),
            ),
            in_specs=[pl.BlockSpec(memory_space=pltpu.HBM)] * 8,
            out_specs=[any_space] * 3,
            scratch_shapes=[
                pltpu.VMEM((width, part), BF16),
                pltpu.VMEM((part, width), BF16),
                pltpu.VMEM((rel_count, width), F32),
                pltpu.VMEM((width, 128), BF16),
                pltpu.VMEM((3, 1, slots), jnp.int32),
                pltpu.VMEM((1, 1), jnp.int32),
                pltpu.VMEM((1, neg_index.shape[1]), jnp.int32),
                pltpu.VMEM((part, 128), F32),
                pltpu.VMEM((n_span, 4, slots), jnp.int32),
                pltpu.VMEM((3, total_edges), jnp.int32),
                pltpu.VMEM((CHUNKS, width, part // CHUNKS), BF16),
                pltpu.VMEM((width, slots), BF16),
                pltpu.VMEM((part, slots), BF16),
                pltpu.VMEM((width, slots), BF16),
                pltpu.VMEM((rel_count, width), F32),
                pltpu.VMEM((width, own), BF16),
                pltpu.VMEM((width, own), F32),
                pltpu.VMEM((width, slots), F32),
                pltpu.VMEM((width, slots), F32),
                pltpu.VMEM((width, slots), F32),
                pltpu.VMEM((width, slots), F32),
                pltpu.VMEM((1, slots), F32),
                pltpu.VMEM((2, 2, rel_rows, width), F32),
                pltpu.VMEM((2, width, own), F32),
                pltpu.VMEM((2, width, own), F32),
                pltpu.VMEM((inner, rel_rows, width), F32),
                pltpu.VMEM((outer, 2 * rel_rows, 256), BF16),
                pltpu.VMEM((rel_rows, width), F32),
                dma((7,)),
                dma((n_span - 1,)),
                dma((n_span,)),
                dma((CHUNKS // 2,)),
                dma((CHUNKS,)),
                dma((CHUNKS // 2,)),
                dma,
                dma,
                dma((4,)),
                dma((4,)),
                dma((inner,)),
                dma((inner,)),
                dma((outer,)),
                dma((outer,)),
                dma((2,)),
            ],
            compiler_params=pltpu.CompilerParams(
                collective_id=0, has_side_effects=True, vmem_limit_bytes=63 * 1024 * 1024
            ),
        )(
            left_emb,
            right_emb,
            relation_weight.T,
            left_index,
            right_index,
            relation_index,
            edge_count,
            neg_index,
        )
        left_grad, right_grad, rel_grad = pl.pallas_call(
            finish,
            out_shape=(
                jax.ShapeDtypeStruct((width, own), F32),
                jax.ShapeDtypeStruct((width, own), F32),
                jax.ShapeDtypeStruct((rel_count, width), F32),
            ),
            in_specs=[any_space] * 3,
            out_specs=[any_space] * 3,
            scratch_shapes=[
                pltpu.VMEM((width, own), F32),
                pltpu.VMEM((width, own), BF16),
                pltpu.VMEM((width, own), F32),
                pltpu.VMEM((rel_count, width), F32),
                dma((6,)),
            ],
        )(left_grad, right_grad, rel_grad.reshape(rel_count, width))
        return left_grad, right_grad, rel_grad.T

    in_specs = (
        P(None, "bucket"),
        P(None, "bucket"),
        P(),
        P("bucket", "span", None),
        P("bucket", "span", None),
        P("bucket", "span", None),
        P("bucket", "span"),
        P("bucket", None),
    )
    out_specs = (P(None, ("bucket", "span")), P(None, ("bucket", "span")), P())
    return jax.shard_map(
        per_device, mesh=mesh, in_specs=in_specs, out_specs=out_specs, check_vma=False
    )
```

```python
import functools
import math

import jax
import jax.numpy as jnp
from jax import lax
from jax.experimental import pallas as pl
from jax.experimental.pallas import tpu as pltpu
from jax.sharding import PartitionSpec as P

MESH = pl.DeviceIdType.MESH
CHUNKS = 4
TILE = 512
F32 = jnp.float32
BF16 = jnp.bfloat16


def nt_dot(a, b):
    return lax.dot_general(a, b, (((1,), (1,)), ((), ())), preferred_element_type=F32)


def dot(a, b):
    return jnp.dot(a, b, preferred_element_type=F32)


def kernel(
    inner,
    left_hbm,
    right_hbm,
    relw_hbm,
    lidx_hbm,
    ridx_hbm,
    relidx_hbm,
    count_hbm,
    neg_hbm,
    left_out,
    right_out,
    rel_out,
    left,
    left_t,
    relw,
    wcat,
    own_idx,
    own_count,
    neg,
    cnt,
    idx_buf,
    edges,
    rbuf,
    query_s,
    w_s,
    rrg_hi,
    rel_acc,
    back_send,
    left_stage,
    right_rows_s,
    left_rows_s,
    rot_s,
    grad_s,
    pos_s,
    rel_part,
    right_part,
    left_part,
    rb1,
    rb2,
    rb3,
    load_sem,
    idx_send,
    idx_recv,
    fwd_send,
    fwd_recv,
    pass_send,
    back_ssem,
    back_rsem,
    part_send,
    part_recv,
    r1_send,
    r1_recv,
    r2_send,
    r2_recv,
    out_sem,
):
    width, part = left.shape
    half = width // 2
    n_bucket = lax.axis_size("bucket")
    n_span = lax.axis_size("span")
    outer = n_bucket // inner
    b = lax.axis_index("bucket")
    s = lax.axis_index("span")
    count_neg = neg.shape[1]
    total_edges = edges.shape[1]
    slots = own_idx.shape[2]
    own_width = part // n_span
    chunk = part // CHUNKS
    core = lax.rem(s, 2)
    sibling = s + 1 - 2 * core
    nxt = lax.rem(b + 1, n_bucket)
    prv = lax.rem(b + n_bucket - 1, n_bucket)
    j = lax.rem(b, inner)
    zi = lax.div(b, inner)

    barrier = pltpu.get_barrier_semaphore()
    peers = [(nxt, s), (prv, s)]
    span_peers = [(b, lax.rem(s + d, n_span)) for d in range(1, n_span)]
    inner_peers = [(zi * inner + lax.rem(j + d, inner), s) for d in range(1, inner)]
    outer_peers = [(lax.rem(zi + d, outer) * inner + j, s) for d in range(1, outer)]
    peers = outer_peers[::-1] + span_peers + inner_peers + peers
    for peer in peers:
        pl.semaphore_signal(barrier, inc=1, device_id=peer, device_id_type=MESH)
    loads = [
        pltpu.make_async_copy(src, dst, load_sem.at[i])
        for i, (src, dst) in enumerate(
            [
                (lidx_hbm.at[0], own_idx.at[0]),
                (ridx_hbm.at[0], own_idx.at[1]),
                (relidx_hbm.at[0], own_idx.at[2]),
                (count_hbm, own_count),
                (neg_hbm, neg),
                (relw_hbm, relw),
                (left_hbm, left),
            ]
        )
    ]
    for load in loads:
        load.start()

    pl.semaphore_wait(barrier, len(peers))

    fwd = []
    for i in range(CHUNKS // 2):
        k = core * (CHUNKS // 2) + i
        fwd.append(
            pltpu.make_async_remote_copy(
                src_ref=right_hbm.at[:, pl.ds(pl.multiple_of(k * chunk, chunk), chunk)],
                dst_ref=rbuf.at[k],
                send_sem=fwd_send.at[i],
                recv_sem=fwd_recv.at[k],
                device_id=(nxt, s),
                device_id_type=MESH,
            )
        )
        fwd[-1].start()

    for load in loads[:4]:
        load.wait()
    slot = lax.broadcasted_iota(jnp.int32, (1, slots), 1)
    live = slot < own_count[...]
    idx_buf[s, 0:1, :] = jnp.where(live, own_idx[0], -1)
    idx_buf[s, 1:2, :] = own_idx[1]
    idx_buf[s, 2:3, :] = own_idx[2]
    idx_buf[s, 3:4, :] = jnp.zeros((1, slots), jnp.int32)

    idx_copies = []
    for d, peer in enumerate(span_peers):
        idx_copies.append(
            pltpu.make_async_remote_copy(
                src_ref=idx_buf.at[s],
                dst_ref=idx_buf.at[s],
                send_sem=idx_send.at[d],
                recv_sem=idx_recv.at[s],
                device_id=peer,
                device_id_type=MESH,
            )
        )
        idx_copies[-1].start()

    loads[4].wait()
    for k in range(part // 128):
        col = lax.broadcasted_iota(jnp.int32, (128, count_neg), 0) + k * 128
        hits = jnp.where(col == neg[...], 1.0, 0.0).astype(F32)
        times = jnp.sum(hits, axis=1, keepdims=True) * (1.0 / count_neg)
        cnt[k * 128 : (k + 1) * 128, :] = jnp.broadcast_to(times, (128, 128))

    loads[5].wait()
    rel_count = relw.shape[0]
    w0 = relw[...]
    w_hi = w0.astype(BF16).astype(F32)
    w_mid = (w0 - w_hi).astype(BF16).astype(F32)
    w_lo = w0 - w_hi - w_mid
    blank = jnp.zeros((128 - 3 * rel_count, width), F32)
    wcat[...] = jnp.concatenate([w_hi, w_mid, w_lo, blank], axis=0).T.astype(BF16)

    loads[6].wait()
    for k in range(part // 128):
        block = left[:, k * 128 : (k + 1) * 128].astype(F32)
        left_t[k * 128 : (k + 1) * 128, :] = block.T.astype(BF16)

    for d in range(1, n_span):
        c = lax.rem(s + d, n_span)
        pltpu.make_async_remote_copy(
            src_ref=idx_buf.at[c],
            dst_ref=idx_buf.at[c],
            send_sem=idx_send.at[d - 1],
            recv_sem=idx_recv.at[c],
            device_id=(b, c),
            device_id_type=MESH,
        ).wait_recv()
    lefts = jnp.concatenate([idx_buf[c, 0:1, :] for c in range(n_span)], axis=0)
    rights = jnp.concatenate([idx_buf[c, 1:2, :] for c in range(n_span)], axis=0)
    kinds = jnp.concatenate([idx_buf[c, 2:3, :] for c in range(n_span)], axis=0)
    sizes = jnp.sum(jnp.where(lefts >= 0, 1.0, 0.0).astype(F32), axis=1, keepdims=True)
    sizes = sizes.astype(jnp.int32)
    begins = [jnp.zeros((1, 1), jnp.int32)]
    for c in range(n_span - 1):
        begins.append(begins[-1] + sizes[c : c + 1])
    start = jnp.concatenate(begins, axis=0)
    bits = (part - 1).bit_length()
    packed = jnp.maximum(lefts, 0) + (rights << bits) + (kinds << (2 * bits))
    packed = jnp.concatenate(
        [packed, jnp.zeros((n_span, total_edges - slots), jnp.int32)], axis=1
    )
    for bit in range((total_edges - 1).bit_length()):
        moved = pltpu.roll(packed, 1 << bit, 1)
        on = jnp.broadcast_to(start & (1 << bit), (n_span, total_edges)) != 0
        packed = jnp.where(on, moved, packed)
    rank = lax.broadcasted_iota(jnp.int32, (n_span, total_edges), 1)
    packed = jnp.where((rank >= start) & (rank < start + sizes), packed, 0)
    line = packed[0:1]
    for c in range(1, n_span):
        line = line + packed[c : c + 1]
    edges[0:1, :] = line & (part - 1)
    edges[1:2, :] = (line >> bits) & (part - 1)
    edges[2:3, :] = line >> (2 * bits)

    core_edges = total_edges // 2
    first = core * core_edges

    for t in range(core_edges // TILE):
        at = slice(t * TILE, (t + 1) * TILE)
        edge_at = pl.ds(pl.multiple_of(first + t * TILE, TILE), TILE)
        kind = lax.broadcasted_iota(jnp.int32, (128, TILE), 0)
        pick_rel = jnp.where((kind & (rel_count - 1)) == edges[2:3, edge_at], 1.0, 0.0).astype(BF16)
        rot_s[:, at] = dot(wcat[...], pick_rel)
        col = lax.broadcasted_iota(jnp.int32, (part, TILE), 0)
        pick = jnp.where(col == edges[0:1, edge_at], 1.0, 0.0).astype(BF16)
        left_rows_s[:, at] = dot(left[...], pick)

    def gather(k, fresh):
        for t in range(core_edges // TILE):
            r_row = edges[1:2, pl.ds(pl.multiple_of(first + t * TILE, TILE), TILE)]
            col = lax.broadcasted_iota(jnp.int32, (chunk, TILE), 0) + k * chunk
            pick = jnp.where(col == r_row, 1.0, 0.0).astype(BF16)
            found = dot(rbuf[k], pick)
            at = slice(t * TILE, (t + 1) * TILE)
            right_rows_s[:, at] = found if fresh else right_rows_s[:, at] + found

    passes = []
    for i in range(CHUNKS // 2):
        k = core * (CHUNKS // 2) + i
        fwd[i].wait_recv()
        passes.append(
            pltpu.make_async_remote_copy(
                src_ref=rbuf.at[k],
                dst_ref=rbuf.at[k],
                send_sem=pass_send.at[i],
                recv_sem=fwd_recv.at[k],
                device_id=(b, sibling),
                device_id_type=MESH,
            )
        )
        passes[-1].start()
        gather(k, i == 0)
    for i in range(CHUNKS // 2):
        k = (1 - core) * (CHUNKS // 2) + i
        pltpu.make_async_remote_copy(
            src_ref=rbuf.at[k],
            dst_ref=rbuf.at[k],
            send_sem=pass_send.at[i],
            recv_sem=fwd_recv.at[k],
            device_id=(b, sibling),
            device_id_type=MESH,
        ).wait_recv()
        gather(k, False)

    rel_acc[...] = jnp.zeros_like(rel_acc)
    own_start = pl.multiple_of(s * own_width, own_width)
    sib_start = pl.multiple_of(sibling * own_width, own_width)

    def tile_step(t):
        at = slice(t * TILE, (t + 1) * TILE)
        edge_at = pl.ds(pl.multiple_of(first + t * TILE, TILE), TILE)
        t_row = edges[2:3, edge_at]
        right_rows = right_rows_s[:, at]
        left_rows = left_rows_s[:, at]
        rot = rot_s[:, at]
        w_re, w_im = rot[:half], rot[half:]
        r_re, r_im = right_rows[:half], right_rows[half:]
        query = jnp.concatenate(
            [w_re * r_re + w_im * r_im, w_re * r_im - w_im * r_re], axis=0
        ).astype(BF16)
        query_s[:, at] = query
        positive = jnp.sum(left_rows * query.astype(F32), axis=0, keepdims=True)
        pos_weight = -1.0 / (1.0 + jnp.exp(positive))
        pos_s[:, at] = pos_weight
        scores = dot(left_t[...], query)
        times = jnp.concatenate([cnt[...]] * (TILE // 128), axis=1)
        weight = (times * pl.reciprocal(1.0 + jnp.exp(-scores), approx=True)).astype(BF16)
        w_s[:, at] = weight
        grad = dot(left[...], weight) + left_rows * pos_weight
        grad_s[:, at] = grad
        a, c = grad[:half], grad[half:]
        turn = jnp.concatenate([a * r_re + c * r_im, a * r_im - c * r_re], axis=0).astype(BF16)
        own_kind = lax.broadcasted_iota(jnp.int32, (rel_count, TILE), 0)
        pick_own = jnp.where(own_kind == t_row, 1.0, 0.0).astype(BF16)
        rel_acc[...] += nt_dot(pick_own, turn)

    for t in range(core_edges // TILE):
        tile_step(t)

    def exchange(buf, me, peers, slots_of, send_sem, recv_sem):
        copies = []
        for d, (peer, other) in enumerate(zip(peers, slots_of)):
            copies.append(
                (
                    pltpu.make_async_remote_copy(
                        src_ref=buf.at[me],
                        dst_ref=buf.at[me],
                        send_sem=send_sem.at[d],
                        recv_sem=recv_sem.at[me],
                        device_id=peer,
                        device_id_type=MESH,
                    ),
                    pltpu.make_async_remote_copy(
                        src_ref=buf.at[other],
                        dst_ref=buf.at[other],
                        send_sem=send_sem.at[d],
                        recv_sem=recv_sem.at[other],
                        device_id=peer,
                        device_id_type=MESH,
                    ),
                )
            )
            copies[-1][0].start()
        return copies

    def to_sibling(i, src, dst):
        copy = pltpu.make_async_remote_copy(
            src_ref=src,
            dst_ref=dst,
            send_sem=part_send.at[i],
            recv_sem=part_recv.at[i],
            device_id=(b, sibling),
            device_id_type=MESH,
        )
        copy.start()
        return copy

    rel_rows = rel_count // 2
    rel_part[0, 0] = rel_acc[0:rel_rows, :]
    rel_part[0, 1] = rel_acc[rel_rows : 2 * rel_rows, :]
    rel_half = to_sibling(0, rel_part.at[0, 1 - core], rel_part.at[1, 0])

    for t in range(core_edges // TILE):
        at = slice(t * TILE, (t + 1) * TILE)
        a, c = grad_s[:half, at], grad_s[half:, at]
        w_re, w_im = rot_s[:half, at], rot_s[half:, at]
        rows = jnp.concatenate([a * w_re - c * w_im, a * w_im + c * w_re], axis=0)
        rrg_hi[:, at] = rows.astype(BF16)
    l_own = edges[0:1, pl.ds(pl.multiple_of(first, core_edges), core_edges)]
    r_own = edges[1:2, pl.ds(pl.multiple_of(first, core_edges), core_edges)]

    def right_columns(start):
        col = lax.broadcasted_iota(jnp.int32, (own_width, core_edges), 0) + start
        pick = jnp.where(col == r_own, 1.0, 0.0).astype(BF16)
        return nt_dot(rrg_hi[...], pick)

    def left_columns(start):
        col = lax.broadcasted_iota(jnp.int32, (own_width, core_edges), 0) + start
        pick = jnp.where(col == l_own, 1.0, 0.0).astype(BF16)
        scaled = query_s[...].astype(F32) * pos_s[...]
        hi = scaled.astype(BF16)
        lo = (scaled - hi.astype(F32)).astype(BF16)
        sums = nt_dot(query_s[...], w_s[pl.ds(start, own_width), :])
        return sums + nt_dot(hi, pick) + nt_dot(lo, pick)

    right_part[0] = right_columns(sib_start)
    right_half = to_sibling(1, right_part.at[0], right_part.at[1])

    rel_half.wait_recv()
    chip_sum = rel_part[0, core] + rel_part[1, 0]
    blank = jnp.zeros((rel_rows, 512 - width), F32)
    lower = jnp.concatenate([chip_sum[:, 256:], blank], axis=1)
    rb1[j] = jnp.concatenate([chip_sum[:, :256], lower], axis=0).astype(BF16)
    stage1 = exchange(
        rb1, j, inner_peers, [lax.rem(j + d, inner) for d in range(1, inner)], r1_send, r1_recv
    )

    right_own = right_columns(own_start)
    right_half.wait_recv()
    back_send[...] = (right_own + right_part[1]).astype(BF16)
    back = pltpu.make_async_remote_copy(
        src_ref=back_send,
        dst_ref=right_out,
        send_sem=back_ssem,
        recv_sem=back_rsem,
        device_id=(prv, s),
        device_id_type=MESH,
    )
    back.start()

    left_part[0] = left_columns(sib_start)
    left_half = to_sibling(2, left_part.at[0], left_part.at[1])

    for _, incoming in stage1:
        incoming.wait_recv()
    rb2[zi] = jnp.sum(rb1[...].astype(F32), axis=0).astype(BF16)
    stage2 = exchange(
        rb2, zi, outer_peers, [lax.rem(zi + d, outer) for d in range(1, outer)], r2_send, r2_recv
    )

    left_own = left_columns(own_start)
    left_half.wait_recv()
    left_stage[...] = left_own + left_part[1]
    left_copy = pltpu.make_async_copy(left_stage, left_out, out_sem.at[0])
    left_copy.start()

    for _, incoming in stage2:
        incoming.wait_recv()
    whole = jnp.sum(rb2[...].astype(F32), axis=0)
    rb3[:, :256] = whole[:rel_rows]
    rb3[:, 256:] = whole[rel_rows:, : width - 256]
    own_rel = pltpu.make_async_copy(rb3, rel_out.at[core], out_sem.at[1])
    own_rel.start()
    rel_whole = to_sibling(3, rb3, rel_out.at[core])
    back.wait_recv()
    pltpu.make_async_remote_copy(
        src_ref=rb3,
        dst_ref=rel_out.at[1 - core],
        send_sem=part_send.at[3],
        recv_sem=part_recv.at[3],
        device_id=(b, sibling),
        device_id_type=MESH,
    ).wait_recv()

    for copy in fwd + idx_copies + passes:
        copy.wait_send()
    back.wait_send()
    for stage in (stage1, stage2):
        for outgoing, _ in stage:
            outgoing.wait_send()
    for copy in (rel_half, right_half, left_half, rel_whole):
        copy.wait_send()
    left_copy.wait()
    own_rel.wait()


def finish(left_in, right_in, rel_in, left_out, right_out, rel_out, left_v, right_b, right_f, rel_v, sems):
    right_copy = pltpu.make_async_copy(right_in, right_b, sems.at[0])
    right_copy.start()
    rel_copy = pltpu.make_async_copy(rel_in, rel_v, sems.at[1])
    rel_copy.start()
    left_copy = pltpu.make_async_copy(left_in, left_v, sems.at[2])
    left_copy.start()
    right_copy.wait()
    right_f[...] = right_b[...].astype(F32)
    right_done = pltpu.make_async_copy(right_f, right_out, sems.at[3])
    right_done.start()
    left_copy.wait()
    left_done = pltpu.make_async_copy(left_v, left_out, sems.at[5])
    left_done.start()
    rel_copy.wait()
    rel_done = pltpu.make_async_copy(rel_v, rel_out, sems.at[4])
    rel_done.start()
    left_done.wait()
    right_done.wait()
    rel_done.wait()


def solution(mesh):
    n_bucket = mesh.shape["bucket"]
    n_span = mesh.shape["span"]
    inner = math.isqrt(n_bucket)
    outer = n_bucket // inner

    def per_device(
        left_emb,
        right_emb,
        relation_weight,
        left_index,
        right_index,
        relation_index,
        edge_count,
        neg_index,
    ):
        width, part = left_emb.shape
        slots = left_index.shape[2]
        total_edges = 2 * slots
        own = part // n_span
        rel_count = relation_weight.shape[1]
        rel_rows = rel_count // 2
        any_space = pl.BlockSpec(memory_space=pl.ANY)
        dma = pltpu.SemaphoreType.DMA
        left_grad, right_grad, rel_grad = pl.pallas_call(
            functools.partial(kernel, inner),
            out_shape=(
                jax.ShapeDtypeStruct((width, own), F32),
                jax.ShapeDtypeStruct((width, own), BF16),
                jax.ShapeDtypeStruct((2, rel_rows, width), F32),
            ),
            in_specs=[pl.BlockSpec(memory_space=pltpu.HBM)] * 8,
            out_specs=[any_space] * 3,
            scratch_shapes=[
                pltpu.VMEM((width, part), BF16),
                pltpu.VMEM((part, width), BF16),
                pltpu.VMEM((rel_count, width), F32),
                pltpu.VMEM((width, 128), BF16),
                pltpu.VMEM((3, 1, slots), jnp.int32),
                pltpu.VMEM((1, 1), jnp.int32),
                pltpu.VMEM((1, neg_index.shape[1]), jnp.int32),
                pltpu.VMEM((part, 128), F32),
                pltpu.VMEM((n_span, 4, slots), jnp.int32),
                pltpu.VMEM((3, total_edges), jnp.int32),
                pltpu.VMEM((CHUNKS, width, part // CHUNKS), BF16),
                pltpu.VMEM((width, slots), BF16),
                pltpu.VMEM((part, slots), BF16),
                pltpu.VMEM((width, slots), BF16),
                pltpu.VMEM((rel_count, width), F32),
                pltpu.VMEM((width, own), BF16),
                pltpu.VMEM((width, own), F32),
                pltpu.VMEM((width, slots), F32),
                pltpu.VMEM((width, slots), F32),
                pltpu.VMEM((width, slots), F32),
                pltpu.VMEM((width, slots), F32),
                pltpu.VMEM((1, slots), F32),
                pltpu.VMEM((2, 2, rel_rows, width), F32),
                pltpu.VMEM((2, width, own), F32),
                pltpu.VMEM((2, width, own), F32),
                pltpu.VMEM((inner, 2 * rel_rows, 256), BF16),
                pltpu.VMEM((outer, 2 * rel_rows, 256), BF16),
                pltpu.VMEM((rel_rows, width), F32),
                dma((7,)),
                dma((n_span - 1,)),
                dma((n_span,)),
                dma((CHUNKS // 2,)),
                dma((CHUNKS,)),
                dma((CHUNKS // 2,)),
                dma,
                dma,
                dma((4,)),
                dma((4,)),
                dma((inner,)),
                dma((inner,)),
                dma((outer,)),
                dma((outer,)),
                dma((2,)),
            ],
            compiler_params=pltpu.CompilerParams(
                collective_id=0, has_side_effects=True, vmem_limit_bytes=63 * 1024 * 1024
            ),
        )(
            left_emb,
            right_emb,
            relation_weight.T,
            left_index,
            right_index,
            relation_index,
            edge_count,
            neg_index,
        )
        left_grad, right_grad, rel_grad = pl.pallas_call(
            finish,
            out_shape=(
                jax.ShapeDtypeStruct((width, own), F32),
                jax.ShapeDtypeStruct((width, own), F32),
                jax.ShapeDtypeStruct((rel_count, width), F32),
            ),
            in_specs=[any_space] * 3,
            out_specs=[any_space] * 3,
            scratch_shapes=[
                pltpu.VMEM((width, own), F32),
                pltpu.VMEM((width, own), BF16),
                pltpu.VMEM((width, own), F32),
                pltpu.VMEM((rel_count, width), F32),
                dma((6,)),
            ],
        )(left_grad, right_grad, rel_grad.reshape(rel_count, width))
        return left_grad, right_grad, rel_grad.T

    in_specs = (
        P(None, "bucket"),
        P(None, "bucket"),
        P(),
        P("bucket", "span", None),
        P("bucket", "span", None),
        P("bucket", "span", None),
        P("bucket", "span"),
        P("bucket", None),
    )
    out_specs = (P(None, ("bucket", "span")), P(None, ("bucket", "span")), P())
    return jax.shard_map(
        per_device, mesh=mesh, in_specs=in_specs, out_specs=out_specs, check_vma=False
    )
```
